128 devices in a mesh: lat: 64 (over z, y, x_hi, core), lon: 2 (over x_lo).
Axes of the slice: x: 4 (x_hi: 2, x_lo: 2; x = x_hi * 2 + x_lo), y: 4, z: 4, core: 2. Of those that a mesh axis runs over, the one named last changes fastest.
Arguments:
- state: bfloat16 [73, 512, 1024], P(None, 'lat', 'lon'), may hold values from -6 to 6
- in_weight: bfloat16 [73, 384], replicated, may hold values from -0.75 to 0.75
- in_bias: float32 [384], replicated, may hold values from -3 to 3
- out_weight: bfloat16 [384, 384], replicated, may hold values from -0.3125 to 0.3125
- out_bias: float32 [384], replicated, may hold values from -3 to 3
- legendre: bfloat16 [256, 2, 512, 512], P('lat', None, 'lon'), may hold values from -0.25 to 0.25
Outputs:
- coefficients: bfloat16 [256, 2, 512, 2, 384], P('lat', None, None, None, 'lon')
The draws below stay inside these ranges and needn't reach their ends.
All inputs are finite; a program needn't handle non-finite values.
Results may differ from the reference program's by a relative error of at most 0.0056.
Values may be sent and summed in bfloat16 or wider, within the bound.
No kernel may reach another device: no remote copies, remote signals or barrier semaphores. Data moves between devices by JAX's collectives and lax.ppermute only.
A program may use at most 64 MiB of HBM per device.

```python
import jax
import jax.numpy as jnp
from jax import lax

CIN = 73
C = 384
NLAT = 512
NLON = 1024
MM = 512


def levels(stream_key, dims, shards, smallest, largest):
    loudness, own = 1.0, jax.random.fold_in(stream_key, 6)
    for axis_at, parts in shards:
        steps = jnp.exp(jax.random.uniform(jax.random.fold_in(own, axis_at), (parts,), jnp.float32, smallest / len(shards), largest / len(shards)))
        loudness = loudness * jnp.repeat(steps, dims[axis_at] // parts).reshape([-1 if axis == axis_at else 1 for axis in range(len(dims))])
    return loudness


def bell_draw(stream_key, dims, width, most, shards=(), held_as=jnp.bfloat16):
    values = jax.random.normal(stream_key, dims, jnp.float32) * width
    if len(shards) > 0:
        values = levels(stream_key, dims, shards, -0.22, 0.18) * values
    return jnp.clip(values, min=-most, max=most).astype(held_as)


def setup_inputs(seed: int = 0) -> dict:
    key_list = jax.random.split(jax.random.key(seed), 7)
    return {
        "state": bell_draw(key_list[0], (CIN, NLAT, NLON), 1.0, 6.0, ((1, 64), (2, 2))),
        "in_weight": bell_draw(key_list[1], (CIN, C), CIN ** -0.5, 0.75),
        "in_bias": bell_draw(key_list[2], (C,), 0.5, 3.0, (), jnp.float32),
        "out_weight": bell_draw(key_list[3], (C, C), C ** -0.5, 0.3125),
        "out_bias": bell_draw(key_list[4], (C,), 0.5, 3.0, (), jnp.float32),
        "legendre": bell_draw(key_list[5], (MM // 2, 2, NLAT, MM), NLAT ** -0.5, 0.25, ((0, 64), (2, 2))),
    }


def order_of(positions):
    pair_index = positions // 2
    member = positions % 2
    return jnp.where(member == 0, pair_index, MM - 1 - pair_index).astype(jnp.int32)

def dft_table():
    orders = order_of(jnp.arange(MM, dtype=jnp.int32))
    columns = jnp.arange(NLON, dtype=jnp.int32)
    phases = columns[:, None] * orders[None, :] % NLON
    angles = phases.astype(jnp.float32) * jnp.float32(2.0 * jnp.pi / NLON)
    factor = jnp.float32(1.0) / jnp.sqrt(jnp.float32(NLON))
    tables = jnp.stack([jnp.cos(angles), -jnp.sin(angles)], axis=1) * factor
    return tables.astype(jnp.bfloat16)

def encode(lat_rows, in_weight, in_bias, out_weight, out_bias):
    hidden = jnp.einsum('cab,ch->hab', lat_rows.astype(jnp.float32), in_weight.astype(jnp.float32))
    hidden = jax.nn.gelu(hidden + in_bias[:, None, None], approximate=False).astype(jnp.bfloat16)
    features = jnp.einsum('hab,hd->dab', hidden.astype(jnp.float32), out_weight.astype(jnp.float32))
    return (features + out_bias[:, None, None]).astype(jnp.bfloat16)

def reference(state, in_weight, in_bias, out_weight, out_bias, legendre):
    tables = dft_table().astype(jnp.float32)
    band = 32
    blocks = state.reshape(CIN, NLAT // band, band, NLON).transpose(1, 0, 2, 3)

    def spectra_block(lat_rows):
        features = encode(lat_rows, in_weight, in_bias, out_weight, out_bias)
        spectra = jnp.einsum('can,nrq->qarc', features.astype(jnp.float32), tables)
        return spectra.astype(jnp.bfloat16)
    spectra = lax.map(spectra_block, blocks)
    spectra = spectra.transpose(1, 0, 2, 3, 4).reshape(MM, NLAT, 2, C)
    weights = legendre.reshape(MM, NLAT, MM)
    orders = order_of(jnp.arange(MM, dtype=jnp.int32))
    degrees = jnp.arange(MM, dtype=jnp.int32)

    def per_order(inputs):
        spectra_one, weights_one, order = inputs
        kept_part = jnp.where(degrees[None, :] >= order, weights_one.astype(jnp.float32), jnp.float32(0.0))
        result = jnp.einsum('kl,krc->lrc', kept_part, spectra_one.astype(jnp.float32))
        return result.astype(jnp.bfloat16)
    coefficients = lax.map(per_order, (spectra, weights, orders))
    return coefficients.reshape(MM // 2, 2, MM, 2, C)
```

```python
import functools

import jax
import jax.numpy as jnp
import numpy as np
from jax import lax
from jax.experimental import pallas as pl
from jax.experimental.pallas import tpu as pltpu
from jax.sharding import PartitionSpec as P

NLON = 1024
HALF = NLON // 2
MM = 512
C = 384
CH = C // 2
OWNERS = 64
PAIRS = 4
LATS = 4
LANE = 128
TILES = MM // LANE
KEPT = (TILES + 1) * LANE
ALL = ("lat", "lon")
MIB = 1 << 20


def dft_tables():
    owner = np.arange(OWNERS)
    columns = np.arange(HALF)
    even, odd = [], []
    for pair in range(PAIRS):
        for member in range(2):
            index = PAIRS * owner + pair
            order = index if member == 0 else MM - 1 - index
            phase = (order[:, None] * columns[None, :]) % NLON
            angle = phase * (2.0 * np.pi / NLON)
            rows = np.stack([np.cos(angle), -np.sin(angle)]) / np.sqrt(float(NLON))
            (even if order[0] % 2 == 0 else odd).append(rows.reshape(2 * OWNERS, HALF))
    return np.stack([np.concatenate(even), np.concatenate(odd)]).astype(np.float32)


def tile_place(packed_tile, block):
    first = TILES - block
    in_first = packed_tile < first
    return jnp.where(in_first, 0, 1), jnp.where(in_first, block + packed_tile, packed_tile - 1)


def order_block():
    return (lax.axis_index("lat") * PAIRS) // LANE


def pack_kernel(legendre_ref, packed_ref):
    block = order_block()
    for tile in range(TILES + 1):
        member, source = tile_place(tile, block)
        start = pl.multiple_of(source * LANE, LANE)
        packed_ref[0, :, tile * LANE:(tile + 1) * LANE] = legendre_ref[0, member, :, pl.ds(start, LANE)]


def pack(legendre):
    rows = legendre.shape[2]
    return pl.pallas_call(
        pack_kernel,
        grid=(PAIRS,),
        in_specs=[pl.BlockSpec((1, 2, rows, MM), lambda i: (i, 0, 0, 0))],
        out_specs=pl.BlockSpec((1, rows, KEPT), lambda i: (i, 0, 0)),
        out_shape=jax.ShapeDtypeStruct((PAIRS, rows, KEPT), jnp.bfloat16),
        cost_estimate=pl.CostEstimate(flops=0, bytes_accessed=4 * MIB, transcendentals=0),
    )(legendre)


def spread_kernel(packed_ref, wide_ref):
    index = lax.axis_index("lat") * PAIRS + pl.program_id(0)
    block = order_block()
    rows = packed_ref.shape[1]
    values = packed_ref[0].astype(jnp.float32).reshape(rows // 8, 8, KEPT)
    lane = lax.broadcasted_iota(jnp.int32, (1, 8, KEPT), 2)
    sub = lax.broadcasted_iota(jnp.int32, (1, 8, KEPT), 1)
    border = (TILES - block) * LANE
    second = lane >= border
    degree = jnp.where(second, lane - LANE, lane + block * LANE)
    order = jnp.where(second, MM - 1 - index, index)
    keep = (degree >= order) & ((sub >= 4) == second)
    swapped = pltpu.roll(values, 4, 1)
    zero = jnp.zeros_like(values)
    upper = jnp.where(keep, jnp.where(second, swapped, values), zero)
    lower = jnp.where(keep, jnp.where(second, values, swapped), zero)
    both = jnp.stack([upper, lower], axis=1)
    wide_ref[0] = both.reshape(2 * rows, KEPT).astype(jnp.bfloat16)


def spread(packed):
    rows = packed.shape[1]
    return pl.pallas_call(
        spread_kernel,
        grid=(PAIRS,),
        in_specs=[pl.BlockSpec((1, rows, KEPT), lambda i: (i, 0, 0))],
        out_specs=pl.BlockSpec((1, 2 * rows, KEPT), lambda i: (i, 0, 0)),
        out_shape=jax.ShapeDtypeStruct((PAIRS, 2 * rows, KEPT), jnp.bfloat16),
        compiler_params=pltpu.CompilerParams(vmem_limit_bytes=32 * MIB),
        cost_estimate=pl.CostEstimate(flops=0, bytes_accessed=4 * MIB, transcendentals=0),
    )(packed)


def gelu(x):
    size = jnp.abs(x)
    t = 1.0 / (1.0 + (0.3275911 * 0.7071067811865476) * size)
    tail = 0.5 * 1.061405429
    for term in (-1.453152027, 1.421413741, -0.284496736, 0.254829592):
        tail = tail * t + 0.5 * term
    tail = tail * t * jnp.exp(-0.5 * x * x)
    return jnp.maximum(x, 0.0) - size * tail


def encode_rows(x, w1, b1, w2, b2):
    contract = (((0,), (0,)), ((), ()))
    hidden = lax.dot_general(x, w1, contract, preferred_element_type=jnp.float32)
    hidden = gelu(hidden + b1).astype(jnp.bfloat16)
    features = jnp.dot(hidden, w2, preferred_element_type=jnp.float32)
    return (features + b2).astype(jnp.bfloat16)


def encode_kernel(x_ref, w1_ref, b1_ref, w2_ref, b2_ref, features_ref):
    row = lax.axis_index("lon") * LATS + pl.program_id(0)
    features_ref[0] = encode_rows(x_ref[row], w1_ref[...], b1_ref[...], w2_ref[...], b2_ref[...])


def whole(array):
    return pl.BlockSpec(array.shape, lambda i: (0,) * array.ndim)


def encode(x, w1, b1, w2, b2):
    return pl.pallas_call(
        encode_kernel,
        grid=(LATS,),
        in_specs=[whole(x), whole(w1), whole(b1), whole(w2), whole(b2)],
        out_specs=pl.BlockSpec((1, HALF, C), lambda i: (i, 0, 0)),
        out_shape=jax.ShapeDtypeStruct((LATS, HALF, C), jnp.bfloat16),
        compiler_params=pltpu.CompilerParams(vmem_limit_bytes=32 * MIB),
        cost_estimate=pl.CostEstimate(flops=2 * LATS * HALF * C * (C + 73), bytes_accessed=4 * MIB,
                                      transcendentals=2 * LATS * HALF * C),
    )(x, w1, b1, w2, b2)


def transform_kernel(x_ref, w1_ref, b1_ref, w2_ref, b2_ref, own_ref, table_ref, out_ref, held):
    lat = pl.program_id(0)
    other = encode_rows(x_ref[0], w1_ref[...], b1_ref[...], w2_ref[...], b2_ref[...]).astype(jnp.float32)
    own = own_ref[0].astype(jnp.float32)
    sign = jnp.where(lax.axis_index("lon") == 0, 1.0, -1.0)
    parts = ((own + other).astype(jnp.bfloat16), (sign * (own - other)).astype(jnp.bfloat16))
    for parity in range(2):
        result = jnp.dot(table_ref[parity], parts[parity], preferred_element_type=jnp.float32)
        for pair in range(PAIRS):
            member = (pair + parity) % 2
            for part in range(2):
                start = (pair * 2 + part) * OWNERS
                rows = pl.ds(member * LATS + lat, OWNERS, stride=2 * LATS)
                for at in range(C // LANE):
                    held[pair * 2 + part, at, rows, :] = (
                        result[start:start + OWNERS, at * LANE:(at + 1) * LANE]
                    )

    @pl.when(lat == LATS - 1)
    def _():
        for pair in range(PAIRS):
            shape = (OWNERS, 2 * LATS, LANE)
            lane = lax.broadcasted_iota(jnp.int32, (OWNERS * 2 * LATS, LANE), 1)
            real_rest = held[pair * 2, 2]
            imag_rest = held[pair * 2 + 1, 2]
            rest = (
                jnp.where(lane < 64, real_rest, pltpu.roll(imag_rest, 64, 1)),
                jnp.where(lane < 64, pltpu.roll(real_rest, 64, 1), imag_rest),
            )
            for side in range(2):
                pieces = (held[pair * 2, side], held[pair * 2 + 1, side], rest[side])
                for at, piece in enumerate(pieces):
                    start = (pair * 3 + at) * LANE
                    out_ref[:, side, :, start:start + LANE] = piece.reshape(shape).astype(jnp.bfloat16)


def transform(x, w1, b1, w2, b2, own, table):
    rows = 2 * LATS
    return pl.pallas_call(
        transform_kernel,
        grid=(LATS,),
        in_specs=[
            pl.BlockSpec((1,) + x.shape[1:], lambda i: (i, 0, 0)),
            whole(w1), whole(b1), whole(w2), whole(b2),
            pl.BlockSpec((1, HALF, C), lambda i: (i, 0, 0)),
            whole(table),
        ],
        out_specs=pl.BlockSpec((OWNERS, 2, rows, PAIRS * C), lambda i: (0, 0, 0, 0)),
        out_shape=jax.ShapeDtypeStruct((OWNERS, 2, rows, PAIRS * C), jnp.bfloat16),
        scratch_shapes=[pltpu.VMEM((2 * PAIRS, C // LANE, OWNERS * rows, LANE), jnp.float32)],
        compiler_params=pltpu.CompilerParams(vmem_limit_bytes=48 * MIB),
        cost_estimate=pl.CostEstimate(flops=2 * LATS * HALF * C * (C + 73 + 2 * MM), bytes_accessed=8 * MIB,
                                      transcendentals=2 * LATS * HALF * C),
    )(x, w1, b1, w2, b2, own, table)


def contract_kernel(spectra_ref, own_ref, other_ref, out_ref):
    half = spectra_ref.shape[0] // 2
    side = lax.axis_index("lon")
    block = order_block()
    dims = (((0,), (0,)), ((), ()))
    mine = spectra_ref[pl.ds(pl.multiple_of(side * half, half), half), :]
    theirs = spectra_ref[pl.ds(pl.multiple_of((1 - side) * half, half), half), :]
    total = lax.dot_general(mine, own_ref[0], dims, preferred_element_type=jnp.float32)
    total += lax.dot_general(theirs, other_ref[0], dims, preferred_element_type=jnp.float32)
    total = total.astype(jnp.bfloat16)
    for tile in range(TILES + 1):
        member, place = tile_place(tile, block)
        lanes = pl.ds(pl.multiple_of(place * LANE, LANE), LANE)
        values = total[:, tile * LANE:(tile + 1) * LANE]
        out_ref[0, member, 0:128, lanes] = values[0:128]
        out_ref[0, member, 192:320, lanes] = values[128:256]
        out_ref[0, member, 128:192, lanes] = values[256:320]
        out_ref[0, member, 320:384, lanes] = values[320:384]
    for tile in range(TILES - 1):
        in_first = tile < block
        member = jnp.where(in_first, 0, 1)
        place = jnp.where(in_first, tile, tile - block)
        lanes = pl.ds(pl.multiple_of(place * LANE, LANE), LANE)
        out_ref[0, member, :, lanes] = jnp.zeros((C, LANE), jnp.bfloat16)


def contract(spectra, own, other):
    rows = spectra.shape[0]
    return pl.pallas_call(
        contract_kernel,
        grid=(PAIRS,),
        in_specs=[
            pl.BlockSpec((rows, C), lambda i: (0, i)),
            pl.BlockSpec((1, rows // 2, KEPT), lambda i: (i, 0, 0)),
            pl.BlockSpec((1, rows // 2, KEPT), lambda i: (i, 0, 0)),
        ],
        out_specs=pl.BlockSpec((1, 2, C, MM), lambda i: (i, 0, 0, 0)),
        out_shape=jax.ShapeDtypeStruct((PAIRS, 2, C, MM), jnp.bfloat16),
        compiler_params=pltpu.CompilerParams(vmem_limit_bytes=48 * MIB),
        cost_estimate=pl.CostEstimate(flops=2 * PAIRS * rows * C * KEPT, bytes_accessed=12 * MIB, transcendentals=0),
    )(spectra, own, other)


def channel_order(array):
    return jnp.concatenate(
        [array[:, 0:128], array[:, 192:320], array[:, 128:192], array[:, 320:384]], axis=1
    )


def shards(state, in_weight, in_bias, out_weight, out_bias, legendre):
    swap = [(0, 1), (1, 0)]
    side = lax.axis_index("lon")
    rows = state.transpose(1, 0, 2)
    sent = lax.dynamic_slice_in_dim(rows, (1 - side) * LATS, LATS, axis=0)
    received = lax.ppermute(sent, "lon", swap)
    weights = (in_weight, in_bias[None, :], channel_order(out_weight), channel_order(out_bias[None, :]))
    own_packed = pack(legendre)
    own = encode(rows, *weights)
    other_packed, received = lax.optimization_barrier((own_packed, received))
    other_packed = lax.ppermute(other_packed, "lon", swap)
    table = jnp.asarray(dft_tables()).astype(jnp.bfloat16)
    spectra = transform(received, *weights, own, table)
    spectra = spectra.reshape(2 * OWNERS * 2 * LATS, PAIRS * C)
    spectra = lax.all_to_all(spectra, ALL, split_axis=0, concat_axis=0, tiled=True)
    result = contract(spectra, spread(own_packed), spread(other_packed))
    return result.reshape(PAIRS, 2, 2, CH, MM).transpose(0, 1, 4, 2, 3)


def solution(mesh):
    return jax.shard_map(
        shards,
        mesh=mesh,
        in_specs=(P(None, "lat", "lon"), P(), P(), P(), P(), P("lat", None, "lon", None)),
        out_specs=P("lat", None, None, None, "lon"),
        check_vma=False,
    )
```

```python
import jax
import jax.numpy as jnp
import numpy as np
from jax import lax
from jax.experimental import pallas as pl
from jax.experimental.pallas import tpu as pltpu
from jax.sharding import PartitionSpec as P

NLON = 1024
HALF = NLON // 2
MM = 512
C = 384
CH = C // 2
OWNERS = 64
PAIRS = 4
LATS = 8
CHUNK = 384
LANE = 128
TILES = MM // LANE
KEPT = (TILES + 1) * LANE
ALL = ("lat", "lon")
MIB = 1 << 20
SMALL = 16 * MIB
MEDIUM = 24 * MIB


def owner_bit(lat):
    return (lat // 2) % 2


def groups():
    return [[2 * lat + (owner_bit(lat) ^ group) for lat in range(OWNERS)] for group in range(2)]


def my_group():
    return owner_bit(lax.axis_index("lat")) ^ lax.axis_index("lon")


def dft_tables():
    columns = np.arange(HALF)
    tables = []
    for parity in range(2):
        rows = []
        for bit in range(2):
            owner = np.array([lat for lat in range(OWNERS) if owner_bit(lat) == bit])
            for pair in range(PAIRS):
                index = PAIRS * owner + pair
                order = index if (pair + parity) % 2 == 0 else MM - 1 - index
                assert np.all(order % 2 == parity)
                phase = (order[:, None] * columns[None, :]) % NLON
                angle = phase * (2.0 * np.pi / NLON)
                rows += [np.cos(angle), -np.sin(angle)]
        tables.append(np.concatenate(rows) / np.sqrt(float(NLON)))
    return np.stack(tables).astype(np.float32)


def tile_place(packed_tile, block):
    in_first = packed_tile < TILES - block
    return jnp.where(in_first, 0, 1), jnp.where(in_first, block + packed_tile, packed_tile - 1)


def order_block():
    return (lax.axis_index("lat") * PAIRS) // LANE


def channel_order(array):
    pieces = [array[:, 0:128], array[:, 192:320], array[:, 128:192], array[:, 320:384]]
    zero = jnp.concatenate(pieces, axis=1)
    one = jnp.concatenate([pieces[1], pieces[0], pieces[3], pieces[2]], axis=1)
    return jnp.where(my_group() == 0, zero, one)


def encode_rows(x, w1, b1, w2, b2):
    hidden = lax.dot_general(x, w1, (((0,), (0,)), ((), ())), preferred_element_type=jnp.float32)
    hidden = hidden + b1
    hidden = (0.5 * hidden) * (1.0 + lax.erf(hidden * np.float32(np.sqrt(0.5))))
    features = jnp.dot(hidden.astype(jnp.bfloat16), w2, preferred_element_type=jnp.float32)
    return (features + b2).astype(jnp.bfloat16)


def pack_copies(legendre_ref, staged, sems):
    block = order_block()
    copies = []
    for tile in range(TILES + 1):
        member, source = tile_place(tile, block)
        lanes = pl.ds(pl.multiple_of(source * LANE, LANE), LANE)
        copies.append(pltpu.make_async_copy(
            legendre_ref.at[:, member, :, lanes],
            staged.at[:, :, tile * LANE:(tile + 1) * LANE],
            sems.at[tile],
        ))
    return copies


def encode_own_kernel(x_ref, w1_hbm, b1_hbm, w2_hbm, b2_hbm, legendre_ref,
                      features_ref, packed_ref, w1_ref, b1_ref, w2_ref, b2_ref,
                      b1_raw, w2_raw, b2_raw, staged, sems, loaded, sent):
    copies = pack_copies(legendre_ref, staged, sems)
    loads = [
        pltpu.make_async_copy(source, target, loaded.at[at])
        for at, (source, target) in enumerate(
            ((w1_hbm, w1_ref), (b1_hbm, b1_raw), (w2_hbm, w2_raw), (b2_hbm, b2_raw)))
    ]
    for load in loads:
        load.start()
    for copy in copies:
        copy.start()
    for load in loads:
        load.wait()
    b1_ref[...] = b1_raw[...][None, :]
    w2_ref[...] = channel_order(w2_raw[...])
    b2_ref[...] = channel_order(b2_raw[...][None, :])
    encode_kernel(x_ref, w1_ref, b1_ref, w2_ref, b2_ref, features_ref)
    result = pltpu.make_async_copy(staged, packed_ref, sent)
    for copy in copies:
        copy.wait()
    result.start()
    result.wait()


def encode_kernel(x_ref, w1_ref, b1_ref, w2_ref, b2_ref, features_ref):
    for lat in range(LATS):
        features_ref[lat] = encode_rows(x_ref[lat], w1_ref[...], b1_ref[...], w2_ref[...], b2_ref[...])


IN_VMEM = pl.BlockSpec(memory_space=pltpu.VMEM)
IN_HBM = pl.BlockSpec(memory_space=pltpu.HBM)


def encode_cost(lats, lons):
    return pl.CostEstimate(flops=2 * lats * lons * C * (C + 73), bytes_accessed=MIB,
                           transcendentals=lats * lons * C)


def combine(own, theirs):
    own, theirs = own.astype(jnp.float32), theirs.astype(jnp.float32)
    sign = jnp.where(lax.axis_index("lon") == 0, 1.0, -1.0)
    return (own + theirs).astype(jnp.bfloat16), (sign * (own - theirs)).astype(jnp.bfloat16)


def first_kernel(x_ref, w1_ref, b1_ref, w2_ref, b2_ref, own_ref, parts_ref):
    lons = x_ref.shape[2]
    for lat in range(LATS):
        theirs = encode_rows(x_ref[lat], w1_ref[...], b1_ref[...], w2_ref[...], b2_ref[...])
        parts_ref[0, lat], parts_ref[1, lat] = combine(own_ref[lat, :lons], theirs)


def first_lons(x, encoder, own):
    lats, _, lons = x.shape
    return pl.pallas_call(
        first_kernel,
        in_specs=[IN_VMEM] * 6,
        out_specs=IN_VMEM,
        out_shape=pltpu.VMEM((2, lats, lons, C), jnp.bfloat16),
        compiler_params=pltpu.CompilerParams(vmem_limit_bytes=SMALL),
        cost_estimate=encode_cost(lats, lons),
    )(x, *encoder, own)


def encode_own(x, w1, b1, w2, b2, legendre):
    lats, _, lons = x.shape
    pairs, _, rows, _ = legendre.shape
    return pl.pallas_call(
        encode_own_kernel,
        in_specs=[IN_VMEM] + [IN_HBM] * 5,
        out_specs=[IN_VMEM, IN_HBM] + [IN_VMEM] * 4,
        out_shape=[
            pltpu.VMEM((lats, lons, C), jnp.bfloat16),
            pltpu.HBM((pairs, rows, KEPT), jnp.bfloat16),
            pltpu.VMEM(w1.shape, jnp.bfloat16),
            pltpu.VMEM((1, C), jnp.float32),
            pltpu.VMEM(w2.shape, jnp.bfloat16),
            pltpu.VMEM((1, C), jnp.float32),
        ],
        scratch_shapes=[
            pltpu.VMEM(b1.shape, jnp.float32),
            pltpu.VMEM(w2.shape, jnp.bfloat16),
            pltpu.VMEM(b2.shape, jnp.float32),
            pltpu.VMEM((pairs, rows, KEPT), jnp.bfloat16),
            pltpu.SemaphoreType.DMA((TILES + 1,)),
            pltpu.SemaphoreType.DMA((4,)),
            pltpu.SemaphoreType.DMA,
        ],
        compiler_params=pltpu.CompilerParams(vmem_limit_bytes=SMALL),
        cost_estimate=encode_cost(lats, lons),
    )(x, w1, b1, w2, b2, legendre)


def transform_kernel(x_ref, w1_ref, b1_ref, w2_ref, b2_ref, own_ref, first_ref, table_ref, out_ref,
                     rest, held, staged, sems):
    lons = x_ref.shape[2]
    for lat in range(LATS):
        theirs = encode_rows(x_ref[lat], w1_ref[...], b1_ref[...], w2_ref[...], b2_ref[...])
        rest[0, lat], rest[1, lat] = combine(own_ref[lat, HALF - lons:], theirs)
    copies = []
    for block in range(4):
        parity, bit = block // 2, block % 2
        spectra_block(parity, bit, table_ref, (first_ref, rest), held.at[block], staged.at[block])
        copies.append(pltpu.make_async_copy(
            staged.at[block],
            out_ref.at[:, bit, :, :, parity * PAIRS * C:(parity + 1) * PAIRS * C],
            sems.at[block],
        ))
        copies[-1].start()
    for copy in copies:
        copy.wait()


def spectra_block(parity, bit, table_ref, parts, held, staged):
    owners = OWNERS // 2
    left = table_ref[parity, bit * 2 * PAIRS * owners:(bit + 1) * 2 * PAIRS * owners, :]
    for lat in range(LATS):
        right = jnp.concatenate([
            jnp.concatenate([part[parity, lat, :, bit * LANE:(bit + 1) * LANE], part[parity, lat, :, 2 * LANE:]], axis=1)
            for part in parts
        ], axis=0)
        result = jnp.dot(left, right, preferred_element_type=jnp.float32)
        rows = pl.ds(lat, owners, stride=LATS)
        for pair in range(PAIRS):
            for angle in range(2):
                start = (pair * 2 + angle) * owners
                for at in range(2):
                    held[pair, angle, at, rows, :] = result[start:start + owners, at * LANE:(at + 1) * LANE]
    lane = lax.broadcasted_iota(jnp.int32, (owners * LATS, LANE), 1)
    for pair in range(PAIRS):
        real = held[pair, 0, 1]
        imag = held[pair, 1, 1]
        if bit == 0:
            imag = pltpu.roll(imag, 64, 1)
        else:
            real = pltpu.roll(real, 64, 1)
        pieces = (held[pair, 0, 0], held[pair, 1, 0], jnp.where(lane < 64, real, imag))
        for at, piece in enumerate(pieces):
            start = (pair * 3 + at) * LANE
            staged[:, :, :, start:start + LANE] = (
                piece.reshape(owners // 2, 2, LATS, LANE).astype(jnp.bfloat16)
            )


def transform(x, encoder, own, first, table):
    return pl.pallas_call(
        transform_kernel,
        in_specs=[IN_VMEM] * 8,
        out_specs=IN_HBM,
        out_shape=pltpu.HBM((OWNERS // 4, 2, 2, LATS, 2 * PAIRS * C), jnp.bfloat16),
        scratch_shapes=[
            pltpu.VMEM((2, LATS, x.shape[2], C), jnp.bfloat16),
            pltpu.VMEM((4, PAIRS, 2, 2, OWNERS // 2 * LATS, LANE), jnp.float32),
            pltpu.VMEM((4, OWNERS // 4, 2, LATS, PAIRS * C), jnp.bfloat16),
            pltpu.SemaphoreType.DMA((4,)),
        ],
        compiler_params=pltpu.CompilerParams(vmem_limit_bytes=MEDIUM),
        cost_estimate=pl.CostEstimate(flops=2 * LATS * HALF * C * (C // 2 + 2 * MM), bytes_accessed=4 * MIB,
                                      transcendentals=LATS * (HALF - CHUNK) * C),
    )(x, *encoder, own, first, table)


def contract_kernel(even_ref, odd_ref, own_ref, packed_ref, out_ref, other):
    half = own_ref.shape[2]
    side = lax.axis_index("lon")
    block = order_block()
    pair = pl.program_id(0)
    index = lax.axis_index("lat") * PAIRS + pair
    mine = pl.ds(pl.multiple_of(side * half, half), half)
    theirs = pl.ds(pl.multiple_of((1 - side) * half, half), half)
    for tile in range(TILES + 1):
        member, place = tile_place(tile, block)
        lanes = pl.ds(pl.multiple_of(place * LANE, LANE), LANE)
        other[member, :, lanes] = packed_ref[0, :, tile * LANE:(tile + 1) * LANE]
    degree = lax.broadcasted_iota(jnp.int32, (C, MM), 1)
    dims = (((0,), (0,)), ((), ()))
    for parity, spectra_ref in enumerate((even_ref, odd_ref)):
        member = (pair + parity) % 2
        order = jnp.where(member == 0, index, MM - 1 - index)
        values = lax.dot_general(
            spectra_ref[mine, :], own_ref[0, member], dims, preferred_element_type=jnp.float32)
        values += lax.dot_general(
            spectra_ref[theirs, :], other[member], dims, preferred_element_type=jnp.float32)
        values = jnp.where(degree >= order, values, 0.0).astype(jnp.bfloat16)
        out_ref[0, member, 0:128] = values[0:128]
        out_ref[0, member, 192:320] = values[128:256]
        out_ref[0, member, 128:192] = values[256:320]
        out_ref[0, member, 320:384] = values[320:384]


def contract(spectra, legendre, packed):
    rows = spectra.shape[0]
    half = legendre.shape[2]
    spectra = pltpu.with_memory_space_constraint(spectra, pltpu.HBM)
    return pl.pallas_call(
        contract_kernel,
        grid=(PAIRS,),
        in_specs=[
            pl.BlockSpec((rows, C), lambda i: (0, i)),
            pl.BlockSpec((rows, C), lambda i: (0, PAIRS + i)),
            pl.BlockSpec((1, 2, half, MM), lambda i: (i, 0, 0, 0)),
            pl.BlockSpec((1, half, KEPT), lambda i: (i, 0, 0)),
        ],
        out_specs=pl.BlockSpec((1, 2, C, MM), lambda i: (i, 0, 0, 0)),
        out_shape=jax.ShapeDtypeStruct((PAIRS, 2, C, MM), jnp.bfloat16),
        scratch_shapes=[pltpu.VMEM((2, half, MM), jnp.bfloat16)],
        compiler_params=pltpu.CompilerParams(vmem_limit_bytes=SMALL),
        cost_estimate=pl.CostEstimate(flops=4 * PAIRS * rows * C * MM, bytes_accessed=12 * MIB, transcendentals=0),
    )(spectra, spectra, legendre, packed)


def by_lat(flat):
    return flat.reshape(-1, LATS, flat.shape[1]).transpose(1, 0, 2)


def shards(state, in_weight, in_bias, out_weight, out_bias, legendre):
    swap = [(0, 1), (1, 0)]
    flat = state.reshape(-1, HALF)
    received = [lax.ppermute(lons, "lon", swap) for lons in (flat[:, :CHUNK], flat[:, CHUNK:])]
    own, packed, *encoder = encode_own(
        by_lat(flat), *(
            pltpu.with_memory_space_constraint(array, pltpu.HBM)
            for array in (in_weight, in_bias, out_weight, out_bias, legendre)))
    first = first_lons(by_lat(received[0]), encoder, own)
    first, last = lax.optimization_barrier((first, received[1]))
    table = jnp.asarray(dft_tables()).astype(jnp.bfloat16)
    spectra = transform(by_lat(last), encoder, own, first, table)
    packed, spectra = lax.optimization_barrier((packed, spectra))
    packed = lax.ppermute(packed, "lon", swap)
    spectra = spectra.reshape(OWNERS, LATS, 2 * PAIRS * C)
    spectra = lax.all_to_all(spectra, ALL, split_axis=0, concat_axis=0, tiled=True, axis_index_groups=groups())
    result = contract(spectra.reshape(OWNERS * LATS, 2 * PAIRS * C), legendre, packed)
    return result.reshape(PAIRS, 2, 2, CH, MM).transpose(0, 1, 4, 2, 3)


def solution(mesh):
    return jax.shard_map(
        shards,
        mesh=mesh,
        in_specs=(P(None, "lat", "lon"), P(), P(), P(), P(), P("lat", None, "lon", None)),
        out_specs=P("lat", None, None, None, "lon"),
        check_vma=False,
    )
```

```python
import jax
import jax.numpy as jnp
import numpy as np
from jax import lax
from jax.experimental import pallas as pl
from jax.experimental.pallas import tpu as pltpu
from jax.sharding import PartitionSpec as P

NLON = 1024
HALF = NLON // 2
MM = 512
C = 384
CH = C // 2
OWNERS = 64
PAIRS = 4
LATS = 8
CHUNK = 384
LANE = 128
OWN_TOGETHER, FIRST_TOGETHER, REST_TOGETHER = 2, 2, 8
TILES = MM // LANE
KEPT = (TILES + 1) * LANE
ALL = ("lat", "lon")
MIB = 1 << 20
SMALL = 16 * MIB
MEDIUM = 24 * MIB


def owner_bit(lat):
    return (lat // 2) % 2


LISTED = [2 * (OWNERS // 2 - 1 - at // 2) + at % 2 for at in range(OWNERS)]


def groups():
    return [[2 * lat + (owner_bit(lat) ^ group) for lat in LISTED] for group in range(2)]


def my_group():
    return owner_bit(lax.axis_index("lat")) ^ lax.axis_index("lon")


def dft_tables():
    columns = np.arange(HALF)
    tables = []
    for parity in range(2):
        rows = []
        for bit in range(2):
            owner = np.array([lat for lat in LISTED if owner_bit(lat) == bit])
            for pair in range(PAIRS):
                index = PAIRS * owner + pair
                order = index if (pair + parity) % 2 == 0 else MM - 1 - index
                assert np.all(order % 2 == parity)
                phase = (order[:, None] * columns[None, :]) % NLON
                angle = phase * (2.0 * np.pi / NLON)
                rows += [np.cos(angle), -np.sin(angle)]
        tables.append(np.concatenate(rows) / np.sqrt(float(NLON)))
    return np.stack(tables).astype(np.float32)


def tile_place(packed_tile, block):
    in_first = packed_tile < TILES - block
    return jnp.where(in_first, 0, 1), jnp.where(in_first, block + packed_tile, packed_tile - 1)


def order_block():
    return (lax.axis_index("lat") * PAIRS) // LANE


def channel_order(array):
    pieces = [array[:, 0:128], array[:, 192:320], array[:, 128:192], array[:, 320:384]]
    zero = jnp.concatenate(pieces, axis=1)
    one = jnp.concatenate([pieces[1], pieces[0], pieces[3], pieces[2]], axis=1)
    return jnp.where(my_group() == 0, zero, one)


def encode_rows(x, w1, b1, w2, b2):
    hidden = lax.dot_general(x, w1, (((0,), (0,)), ((), ())), preferred_element_type=jnp.float32)
    hidden = hidden + b1
    hidden = (0.5 * hidden) * (1.0 + lax.erf(hidden * np.float32(np.sqrt(0.5))))
    features = jnp.dot(hidden.astype(jnp.bfloat16), w2, preferred_element_type=jnp.float32)
    return (features + b2).astype(jnp.bfloat16)


def pack_copies(legendre_ref, staged, sems):
    block = order_block()
    copies = []
    for tile in range(TILES + 1):
        member, source = tile_place(tile, block)
        lanes = pl.ds(pl.multiple_of(source * LANE, LANE), LANE)
        copies.append(pltpu.make_async_copy(
            legendre_ref.at[:, member, :, lanes],
            staged.at[:, :, tile * LANE:(tile + 1) * LANE],
            sems.at[tile],
        ))
    return copies


def encode_own_kernel(x_ref, w1_hbm, b1_hbm, w2_hbm, b2_hbm, legendre_ref,
                      features_ref, packed_ref, w1_ref, b1_ref, w2_ref, b2_ref,
                      b1_raw, w2_raw, b2_raw, staged, sems, loaded, sent):
    copies = pack_copies(legendre_ref, staged, sems)
    loads = [
        pltpu.make_async_copy(source, target, loaded.at[at])
        for at, (source, target) in enumerate(
            ((w1_hbm, w1_ref), (b1_hbm, b1_raw), (w2_hbm, w2_raw), (b2_hbm, b2_raw)))
    ]
    for load in loads:
        load.start()
    for copy in copies:
        copy.start()
    for load in loads:
        load.wait()
    b1_ref[...] = b1_raw[...][None, :]
    w2_ref[...] = channel_order(w2_raw[...])
    b2_ref[...] = channel_order(b2_raw[...][None, :])
    for lat, features in encode_lats(x_ref, w1_ref, b1_ref, w2_ref, b2_ref, OWN_TOGETHER):
        features_ref[lat] = features
    result = pltpu.make_async_copy(staged, packed_ref, sent)
    for copy in copies:
        copy.wait()
    result.start()
    result.wait()


def encode_lats(x_ref, w1_ref, b1_ref, w2_ref, b2_ref, together):
    lons = x_ref.shape[1] // LATS
    for lat in range(0, LATS, together):
        features = encode_rows(
            x_ref[:, lat * lons:(lat + together) * lons], w1_ref[...], b1_ref[...], w2_ref[...], b2_ref[...])
        for at in range(together):
            yield lat + at, features[at * lons:(at + 1) * lons]


IN_VMEM = pl.BlockSpec(memory_space=pltpu.VMEM)
IN_HBM = pl.BlockSpec(memory_space=pltpu.HBM)


def encode_cost(lats, lons):
    return pl.CostEstimate(flops=2 * lats * lons * C * (C + 73), bytes_accessed=MIB,
                           transcendentals=lats * lons * C)


def combine(own, theirs):
    own, theirs = own.astype(jnp.float32), theirs.astype(jnp.float32)
    sign = jnp.where(lax.axis_index("lon") == 0, 1.0, -1.0)
    return (own + theirs).astype(jnp.bfloat16), (sign * (own - theirs)).astype(jnp.bfloat16)


def first_kernel(x_ref, w1_ref, b1_ref, w2_ref, b2_ref, own_ref, parts_ref):
    lons = x_ref.shape[1] // LATS
    for lat, theirs in encode_lats(x_ref, w1_ref, b1_ref, w2_ref, b2_ref, FIRST_TOGETHER):
        parts_ref[0, lat], parts_ref[1, lat] = combine(own_ref[lat, :lons], theirs)


def first_lons(x, encoder, own):
    lats, lons = LATS, x.shape[1] // LATS
    return pl.pallas_call(
        first_kernel,
        in_specs=[IN_VMEM] * 6,
        out_specs=IN_VMEM,
        out_shape=pltpu.VMEM((2, lats, lons, C), jnp.bfloat16),
        compiler_params=pltpu.CompilerParams(vmem_limit_bytes=SMALL),
        cost_estimate=encode_cost(lats, lons),
    )(x, *encoder, own)


def encode_own(x, w1, b1, w2, b2, legendre):
    lats, lons = LATS, x.shape[1] // LATS
    pairs, _, rows, _ = legendre.shape
    return pl.pallas_call(
        encode_own_kernel,
        in_specs=[IN_VMEM] + [IN_HBM] * 5,
        out_specs=[IN_VMEM, IN_HBM] + [IN_VMEM] * 4,
        out_shape=[
            pltpu.VMEM((lats, lons, C), jnp.bfloat16),
            pltpu.HBM((pairs, rows, KEPT), jnp.bfloat16),
            pltpu.VMEM(w1.shape, jnp.bfloat16),
            pltpu.VMEM((1, C), jnp.float32),
            pltpu.VMEM(w2.shape, jnp.bfloat16),
            pltpu.VMEM((1, C), jnp.float32),
        ],
        scratch_shapes=[
            pltpu.VMEM(b1.shape, jnp.float32),
            pltpu.VMEM(w2.shape, jnp.bfloat16),
            pltpu.VMEM(b2.shape, jnp.float32),
            pltpu.VMEM((pairs, rows, KEPT), jnp.bfloat16),
            pltpu.SemaphoreType.DMA((TILES + 1,)),
            pltpu.SemaphoreType.DMA((4,)),
            pltpu.SemaphoreType.DMA,
        ],
        compiler_params=pltpu.CompilerParams(vmem_limit_bytes=SMALL),
        cost_estimate=encode_cost(lats, lons),
    )(x, w1, b1, w2, b2, legendre)


def transform_kernel(x_ref, w1_ref, b1_ref, w2_ref, b2_ref, own_ref, first_ref, table_ref, out_ref,
                     rest, held, staged, sems):
    lons = x_ref.shape[1] // LATS
    for lat, theirs in encode_lats(x_ref, w1_ref, b1_ref, w2_ref, b2_ref, REST_TOGETHER):
        rest[0, lat], rest[1, lat] = combine(own_ref[lat, HALF - lons:], theirs)
    copies = []
    for block in range(4):
        parity, bit = block // 2, block % 2
        spectra_block(parity, bit, table_ref, (first_ref, rest), held.at[block])
        for pair in range(PAIRS):
            arrange(bit, held.at[block, pair], staged.at[block, pair])
            slot = parity * PAIRS + pair
            copies.append(pltpu.make_async_copy(
                staged.at[block, pair],
                out_ref.at[:, 1 - bit, :, :, slot * C:(slot + 1) * C],
                sems.at[block, pair],
            ))
            copies[-1].start()
    for copy in copies:
        copy.wait()


def spectra_block(parity, bit, table_ref, parts, held):
    owners = OWNERS // 2
    left = table_ref[parity, bit * 2 * PAIRS * owners:(bit + 1) * 2 * PAIRS * owners, :]
    for lat in range(LATS):
        right = jnp.concatenate([
            jnp.concatenate([part[parity, lat, :, bit * LANE:(bit + 1) * LANE], part[parity, lat, :, 2 * LANE:]], axis=1)
            for part in parts
        ], axis=0)
        result = jnp.dot(left, right, preferred_element_type=jnp.float32)
        rows = pl.ds(lat, owners, stride=LATS)
        for pair in range(PAIRS):
            for angle in range(2):
                start = (pair * 2 + angle) * owners
                for at in range(2):
                    held[pair, angle, at, rows, :] = result[start:start + owners, at * LANE:(at + 1) * LANE]


def arrange(bit, held, staged):
    real, imag = held[0, 1], held[1, 1]
    if bit == 0:
        imag = pltpu.roll(imag, 64, 1)
    else:
        real = pltpu.roll(real, 64, 1)
    lane = lax.broadcasted_iota(jnp.int32, real.shape, 1)
    for at, piece in enumerate((held[0, 0], held[1, 0], jnp.where(lane < 64, real, imag))):
        staged[:, :, :, at * LANE:(at + 1) * LANE] = piece.reshape(-1, 2, LATS, LANE).astype(jnp.bfloat16)


def transform(x, encoder, own, first, table):
    return pl.pallas_call(
        transform_kernel,
        in_specs=[IN_VMEM] * 8,
        out_specs=IN_HBM,
        out_shape=pltpu.HBM((OWNERS // 4, 2, 2, LATS, 2 * PAIRS * C), jnp.bfloat16),
        scratch_shapes=[
            pltpu.VMEM((2, LATS, x.shape[1] // LATS, C), jnp.bfloat16),
            pltpu.VMEM((4, PAIRS, 2, 2, OWNERS // 2 * LATS, LANE), jnp.float32),
            pltpu.VMEM((4, PAIRS, OWNERS // 4, 2, LATS, C), jnp.bfloat16),
            pltpu.SemaphoreType.DMA((4, PAIRS)),
        ],
        compiler_params=pltpu.CompilerParams(vmem_limit_bytes=MEDIUM),
        cost_estimate=pl.CostEstimate(flops=2 * LATS * HALF * C * (C // 2 + 2 * MM), bytes_accessed=4 * MIB,
                                      transcendentals=LATS * (HALF - CHUNK) * C),
    )(x, *encoder, own, first, table)


def contract_kernel(spectra_ref, own_ref, packed_ref, out_ref, other, spectra, staged, read, written):
    half = own_ref.shape[2]
    reads = []
    for slot in range(2 * PAIRS):
        lanes = slice(slot * C, (slot + 1) * C)
        reads.append(pltpu.make_async_copy(spectra_ref.at[:, lanes], spectra.at[:, lanes], read.at[slot]))
    for pair in range(PAIRS):
        reads[pair].start()
        reads[PAIRS + pair].start()
    side = lax.axis_index("lon")
    block = order_block()
    for tile in range(TILES + 1):
        member, place = tile_place(tile, block)
        lanes = pl.ds(pl.multiple_of(place * LANE, LANE), LANE)
        for pair in range(PAIRS):
            other[pair, member, :, lanes] = packed_ref[pair, :, tile * LANE:(tile + 1) * LANE]

    def products(full):
        writes = []
        for pair in range(PAIRS):
            index = lax.axis_index("lat") * PAIRS + pair
            reads[pair].wait()
            reads[PAIRS + pair].wait()
            for member in range(2):
                slot = (pair + member) % 2 * PAIRS + pair
                start = 0 if member == full else MM // 2
                order = MM - 1 - index if member else index
                values = 0.0
                for which, held in ((side, own_ref), (1 - side, other)):
                    values += lax.dot_general(
                        by_latitude(spectra, which, half, slot), held[pair, member, :, start:],
                        (((0,), (0,)), ((), ())), preferred_element_type=jnp.float32)
                degree = lax.broadcasted_iota(jnp.int32, values.shape, 1) + start
                values = jnp.where(degree >= order, values, 0.0).astype(jnp.bfloat16)
                for at, to, count in ((0, 0, 128), (128, 192, 128), (256, 128, 64), (320, 320, 64)):
                    staged[slot, to:to + count, start:] = values[at:at + count]
                if start:
                    staged[slot, :, :start] = jnp.zeros((C, start), jnp.bfloat16)
                writes.append(pltpu.make_async_copy(staged.at[slot], out_ref.at[pair, member], written.at[slot]))
                writes[-1].start()
        for write in writes:
            write.wait()

    for full in range(2):
        pl.when((block < TILES // 2) == (full == 0))(lambda full=full: products(full))


def by_latitude(spectra, which, half, slot):
    last = (1 - which) * half + half - 16
    return jnp.concatenate([
        spectra[pl.ds(pl.multiple_of(last - at, 16), 16), slot * C:(slot + 1) * C] for at in range(0, half, 16)
    ], axis=0)


def contract(spectra, legendre, packed):
    half = legendre.shape[2]
    spectra = pltpu.with_memory_space_constraint(spectra, pltpu.HBM)
    return pl.pallas_call(
        contract_kernel,
        in_specs=[IN_HBM, IN_VMEM, IN_VMEM],
        out_specs=IN_HBM,
        out_shape=pltpu.HBM((PAIRS, 2, C, MM), jnp.bfloat16),
        scratch_shapes=[
            pltpu.VMEM((PAIRS, 2, half, MM), jnp.bfloat16),
            pltpu.VMEM(spectra.shape, jnp.bfloat16),
            pltpu.VMEM((2 * PAIRS, C, MM), jnp.bfloat16),
            pltpu.SemaphoreType.DMA((2 * PAIRS,)),
            pltpu.SemaphoreType.DMA((2 * PAIRS,)),
        ],
        compiler_params=pltpu.CompilerParams(vmem_limit_bytes=MEDIUM),
        cost_estimate=pl.CostEstimate(flops=8 * PAIRS * half * C * MM, bytes_accessed=8 * MIB, transcendentals=0),
    )(spectra, legendre, packed)


def by_lat(flat):
    return flat.reshape(-1, LATS * flat.shape[1])


def shards(state, in_weight, in_bias, out_weight, out_bias, legendre):
    swap = [(0, 1), (1, 0)]
    flat = state.reshape(-1, HALF)
    received = [lax.ppermute(flat[:, :CHUNK], "lon", swap)]
    own, packed, *encoder = encode_own(
        by_lat(flat), *(
            pltpu.with_memory_space_constraint(array, pltpu.HBM)
            for array in (in_weight, in_bias, out_weight, out_bias, legendre)))
    rest, own = lax.optimization_barrier((flat[:, CHUNK:], own))
    received.append(lax.ppermute(rest, "lon", swap))
    first = first_lons(by_lat(received[0]), encoder, own)
    first, last = lax.optimization_barrier((first, received[1]))
    table = jnp.asarray(dft_tables()).astype(jnp.bfloat16)
    spectra = transform(by_lat(last), encoder, own, first, table)
    packed, spectra = lax.optimization_barrier((packed, spectra))
    packed = lax.ppermute(packed, "lon", swap)
    spectra = spectra.reshape(OWNERS, LATS, 2 * PAIRS * C)
    spectra = lax.all_to_all(spectra, ALL, split_axis=0, concat_axis=0, tiled=True, axis_index_groups=groups())
    result = contract(spectra.reshape(OWNERS * LATS, 2 * PAIRS * C), legendre, packed)
    return result.reshape(PAIRS, 2, 2, CH, MM).transpose(0, 1, 4, 2, 3)


def solution(mesh):
    return jax.shard_map(
        shards,
        mesh=mesh,
        in_specs=(P(None, "lat", "lon"), P(), P(), P(), P(), P("lat", None, "lon", None)),
        out_specs=P("lat", None, None, None, "lon"),
        check_vma=False,
    )
```

```python
import jax
import jax.numpy as jnp
import numpy as np
from jax import lax
from jax.experimental import pallas as pl
from jax.experimental.pallas import tpu as pltpu
from jax.sharding import PartitionSpec as P

NLON = 1024
HALF = NLON // 2
MM = 512
C = 384
CH = C // 2
OWNERS = 64
PAIRS = 4
LATS = 8
CHUNK = 384
LANE = 128
OWN_TOGETHER, FIRST_TOGETHER, REST_TOGETHER = 2, 2, 8
TILES = MM // LANE
KEPT = (TILES + 1) * LANE
ALL = ("lat", "lon")
MIB = 1 << 20
SMALL = 16 * MIB
MEDIUM = 24 * MIB


def owner_bit(lat):
    return (lat // 2) % 2


PLACES = [4 * z + y for y in range(3, -1, -1) for z in range(3, -1, -1)]
BITS = (0, 1)
LISTED = [4 * place + 2 * bit + core for place in PLACES for bit in BITS for core in range(2)]


def groups():
    return [[2 * lat + (owner_bit(lat) ^ group) for lat in LISTED] for group in range(2)]


def my_group():
    return owner_bit(lax.axis_index("lat")) ^ lax.axis_index("lon")


def dft_tables():
    columns = np.arange(HALF)
    tables = []
    for parity in range(2):
        rows = []
        for bit in range(2):
            owner = np.array([lat for lat in LISTED if owner_bit(lat) == bit])
            for pair in range(PAIRS):
                index = PAIRS * owner + pair
                order = index if (pair + parity) % 2 == 0 else MM - 1 - index
                assert np.all(order % 2 == parity)
                phase = (order[:, None] * columns[None, :]) % NLON
                angle = phase * (2.0 * np.pi / NLON)
                rows += [np.cos(angle), -np.sin(angle)]
        tables.append(np.concatenate(rows) / np.sqrt(float(NLON)))
    return np.stack(tables).astype(np.float32)


def tile_place(packed_tile, block):
    in_first = packed_tile < TILES - block
    return jnp.where(in_first, 0, 1), jnp.where(in_first, block + packed_tile, packed_tile - 1)


def order_block():
    return (lax.axis_index("lat") * PAIRS) // LANE


def channel_order(array):
    pieces = [array[:, 0:128], array[:, 192:320], array[:, 128:192], array[:, 320:384]]
    zero = jnp.concatenate(pieces, axis=1)
    one = jnp.concatenate([pieces[1], pieces[0], pieces[3], pieces[2]], axis=1)
    return jnp.where(my_group() == 0, zero, one)


def encode_rows(x, w1, b1, w2, b2):
    hidden = lax.dot_general(x, w1, (((0,), (0,)), ((), ())), preferred_element_type=jnp.float32)
    hidden = hidden + b1
    hidden = (0.5 * hidden) * (1.0 + lax.erf(hidden * np.float32(np.sqrt(0.5))))
    features = jnp.dot(hidden.astype(jnp.bfloat16), w2, preferred_element_type=jnp.float32)
    return (features + b2).astype(jnp.bfloat16)


def pack_copies(legendre_ref, staged, sems):
    block = order_block()
    copies = []
    for tile in range(TILES + 1):
        member, source = tile_place(tile, block)
        lanes = pl.ds(pl.multiple_of(source * LANE, LANE), LANE)
        copies.append(pltpu.make_async_copy(
            legendre_ref.at[:, member, :, lanes],
            staged.at[:, :, tile * LANE:(tile + 1) * LANE],
            sems.at[tile],
        ))
    return copies


def encode_own_kernel(x_ref, w1_hbm, b1_hbm, w2_hbm, b2_hbm, legendre_ref,
                      features_ref, packed_ref, w1_ref, b1_ref, w2_ref, b2_ref,
                      b1_raw, w2_raw, b2_raw, staged, sems, loaded, sent):
    copies = pack_copies(legendre_ref, staged, sems)
    loads = [
        pltpu.make_async_copy(source, target, loaded.at[at])
        for at, (source, target) in enumerate(
            ((w1_hbm, w1_ref), (b1_hbm, b1_raw), (w2_hbm, w2_raw), (b2_hbm, b2_raw)))
    ]
    for load in loads:
        load.start()
    for copy in copies:
        copy.start()
    for load in loads:
        load.wait()
    b1_ref[...] = b1_raw[...][None, :]
    w2_ref[...] = channel_order(w2_raw[...])
    b2_ref[...] = channel_order(b2_raw[...][None, :])
    for lat, features in encode_lats(x_ref, w1_ref, b1_ref, w2_ref, b2_ref, OWN_TOGETHER):
        features_ref[lat] = features
    result = pltpu.make_async_copy(staged, packed_ref, sent)
    for copy in copies:
        copy.wait()
    result.start()
    result.wait()


def encode_lats(x_ref, w1_ref, b1_ref, w2_ref, b2_ref, together):
    lons = x_ref.shape[2]
    for lat in range(0, LATS, together):
        rows = jnp.concatenate([x_ref[lat + at] for at in range(together)], axis=1)
        features = encode_rows(rows, w1_ref[...], b1_ref[...], w2_ref[...], b2_ref[...])
        for at in range(together):
            yield lat + at, features[at * lons:(at + 1) * lons]


IN_VMEM = pl.BlockSpec(memory_space=pltpu.VMEM)
IN_HBM = pl.BlockSpec(memory_space=pltpu.HBM)


def encode_cost(lats, lons):
    return pl.CostEstimate(flops=2 * lats * lons * C * (C + 73), bytes_accessed=MIB,
                           transcendentals=lats * lons * C)


def combine(own, theirs):
    own, theirs = own.astype(jnp.float32), theirs.astype(jnp.float32)
    sign = jnp.where(lax.axis_index("lon") == 0, 1.0, -1.0)
    return (own + theirs).astype(jnp.bfloat16), (sign * (own - theirs)).astype(jnp.bfloat16)


def first_kernel(x_ref, w1_ref, b1_ref, w2_ref, b2_ref, own_ref, parts_ref):
    lons = x_ref.shape[2]
    for lat, theirs in encode_lats(x_ref, w1_ref, b1_ref, w2_ref, b2_ref, FIRST_TOGETHER):
        parts_ref[0, lat], parts_ref[1, lat] = combine(own_ref[lat, :lons], theirs)


def first_lons(x, encoder, own):
    lats, _, lons = x.shape
    return pl.pallas_call(
        first_kernel,
        in_specs=[IN_VMEM] * 6,
        out_specs=IN_VMEM,
        out_shape=pltpu.VMEM((2, lats, lons, C), jnp.bfloat16),
        compiler_params=pltpu.CompilerParams(vmem_limit_bytes=SMALL),
        cost_estimate=encode_cost(lats, lons),
    )(x, *encoder, own)


def encode_own(x, w1, b1, w2, b2, legendre):
    lats, _, lons = x.shape
    pairs, _, rows, _ = legendre.shape
    return pl.pallas_call(
        encode_own_kernel,
        in_specs=[IN_VMEM] + [IN_HBM] * 5,
        out_specs=[IN_VMEM, IN_HBM] + [IN_VMEM] * 4,
        out_shape=[
            pltpu.VMEM((lats, lons, C), jnp.bfloat16),
            pltpu.HBM((pairs, rows, KEPT), jnp.bfloat16),
            pltpu.VMEM(w1.shape, jnp.bfloat16),
            pltpu.VMEM((1, C), jnp.float32),
            pltpu.VMEM(w2.shape, jnp.bfloat16),
            pltpu.VMEM((1, C), jnp.float32),
        ],
        scratch_shapes=[
            pltpu.VMEM(b1.shape, jnp.float32),
            pltpu.VMEM(w2.shape, jnp.bfloat16),
            pltpu.VMEM(b2.shape, jnp.float32),
            pltpu.VMEM((pairs, rows, KEPT), jnp.bfloat16),
            pltpu.SemaphoreType.DMA((TILES + 1,)),
            pltpu.SemaphoreType.DMA((4,)),
            pltpu.SemaphoreType.DMA,
        ],
        compiler_params=pltpu.CompilerParams(vmem_limit_bytes=SMALL),
        cost_estimate=encode_cost(lats, lons),
    )(x, w1, b1, w2, b2, legendre)


def transform_kernel(x_ref, w1_ref, b1_ref, w2_ref, b2_ref, own_ref, first_ref, table_ref, out_ref,
                     rest, held, staged, sems):
    lons = x_ref.shape[2]
    for lat, theirs in encode_lats(x_ref, w1_ref, b1_ref, w2_ref, b2_ref, REST_TOGETHER):
        rest[0, lat], rest[1, lat] = combine(own_ref[lat, HALF - lons:], theirs)
    copies = []
    for block in range(4):
        parity, bit = block // 2, block % 2
        spectra_block(parity, bit, table_ref, (first_ref, rest), held.at[block])
        for pair in range(PAIRS):
            arrange(bit, held.at[block, pair], staged.at[block, pair])
            slot = parity * PAIRS + pair
            copies.append(pltpu.make_async_copy(
                staged.at[block, pair],
                out_ref.at[:, BITS.index(bit), :, :, slot * C:(slot + 1) * C],
                sems.at[block, pair],
            ))
            copies[-1].start()
    for copy in copies:
        copy.wait()


def spectra_block(parity, bit, table_ref, parts, held):
    owners = OWNERS // 2
    left = table_ref[parity, bit * 2 * PAIRS * owners:(bit + 1) * 2 * PAIRS * owners, :]
    for lat in range(LATS):
        right = jnp.concatenate([
            jnp.concatenate([part[parity, lat, :, bit * LANE:(bit + 1) * LANE], part[parity, lat, :, 2 * LANE:]], axis=1)
            for part in parts
        ], axis=0)
        result = jnp.dot(left, right, preferred_element_type=jnp.float32)
        rows = pl.ds(lat, owners, stride=LATS)
        for pair in range(PAIRS):
            for angle in range(2):
                start = (pair * 2 + angle) * owners
                for at in range(2):
                    held[pair, angle, at, rows, :] = result[start:start + owners, at * LANE:(at + 1) * LANE]


def arrange(bit, held, staged):
    real, imag = held[0, 1], held[1, 1]
    if bit == 0:
        imag = pltpu.roll(imag, 64, 1)
    else:
        real = pltpu.roll(real, 64, 1)
    lane = lax.broadcasted_iota(jnp.int32, real.shape, 1)
    for at, piece in enumerate((held[0, 0], held[1, 0], jnp.where(lane < 64, real, imag))):
        staged[:, :, :, at * LANE:(at + 1) * LANE] = piece.reshape(-1, 2, LATS, LANE).astype(jnp.bfloat16)


def transform(x, encoder, own, first, table):
    return pl.pallas_call(
        transform_kernel,
        in_specs=[IN_VMEM] * 8,
        out_specs=IN_HBM,
        out_shape=pltpu.HBM((OWNERS // 4, 2, 2, LATS, 2 * PAIRS * C), jnp.bfloat16),
        scratch_shapes=[
            pltpu.VMEM((2, LATS, x.shape[2], C), jnp.bfloat16),
            pltpu.VMEM((4, PAIRS, 2, 2, OWNERS // 2 * LATS, LANE), jnp.float32),
            pltpu.VMEM((4, PAIRS, OWNERS // 4, 2, LATS, C), jnp.bfloat16),
            pltpu.SemaphoreType.DMA((4, PAIRS)),
        ],
        compiler_params=pltpu.CompilerParams(vmem_limit_bytes=MEDIUM),
        cost_estimate=pl.CostEstimate(flops=2 * LATS * HALF * C * (C // 2 + 2 * MM), bytes_accessed=4 * MIB,
                                      transcendentals=LATS * (HALF - CHUNK) * C),
    )(x, *encoder, own, first, table)


def contract_kernel(spectra_ref, own_ref, packed_ref, out_ref, other, spectra, staged, read, written):
    half = own_ref.shape[2]
    reads = []
    for slot in range(2 * PAIRS):
        lanes = slice(slot * C, (slot + 1) * C)
        reads.append(pltpu.make_async_copy(spectra_ref.at[:, lanes], spectra.at[:, lanes], read.at[slot]))
    for pair in range(PAIRS):
        reads[pair].start()
        reads[PAIRS + pair].start()
    side = lax.axis_index("lon")
    block = order_block()
    for tile in range(TILES + 1):
        member, place = tile_place(tile, block)
        lanes = pl.ds(pl.multiple_of(place * LANE, LANE), LANE)
        for pair in range(PAIRS):
            other[pair, member, :, lanes] = packed_ref[pair, :, tile * LANE:(tile + 1) * LANE]

    def products(full):
        writes = []
        for pair in range(PAIRS):
            index = lax.axis_index("lat") * PAIRS + pair
            reads[pair].wait()
            reads[PAIRS + pair].wait()
            for member in range(2):
                slot = (pair + member) % 2 * PAIRS + pair
                start = 0 if member == full else MM // 2
                order = MM - 1 - index if member else index
                values = 0.0
                for which, held in ((side, own_ref), (1 - side, other)):
                    values += lax.dot_general(
                        by_latitude(spectra, which, half, slot), held[pair, member, :, start:],
                        (((0,), (0,)), ((), ())), preferred_element_type=jnp.float32)
                degree = lax.broadcasted_iota(jnp.int32, values.shape, 1) + start
                values = jnp.where(degree >= order, values, 0.0).astype(jnp.bfloat16)
                for at, to, count in ((0, 0, 128), (128, 192, 128), (256, 128, 64), (320, 320, 64)):
                    staged[slot, to:to + count, start:] = values[at:at + count]
                if start:
                    staged[slot, :, :start] = jnp.zeros((C, start), jnp.bfloat16)
                writes.append(pltpu.make_async_copy(staged.at[slot], out_ref.at[pair, member], written.at[slot]))
                writes[-1].start()
        for write in writes:
            write.wait()

    for full in range(2):
        pl.when((block < TILES // 2) == (full == 0))(lambda full=full: products(full))


def by_latitude(spectra, which, half, slot):
    pieces = []
    for at in range(half // 16):
        first, second = (LISTED.index(2 * index) // 2 for index in (at, at + half // 16))
        start = pl.multiple_of(16 * jnp.where(which == 0, first, second), 16)
        pieces.append(spectra[pl.ds(start, 16), slot * C:(slot + 1) * C])
    return jnp.concatenate(pieces, axis=0)


def contract(spectra, legendre, packed):
    half = legendre.shape[2]
    spectra = pltpu.with_memory_space_constraint(spectra, pltpu.HBM)
    return pl.pallas_call(
        contract_kernel,
        in_specs=[IN_HBM, IN_VMEM, IN_VMEM],
        out_specs=IN_HBM,
        out_shape=pltpu.HBM((PAIRS, 2, C, MM), jnp.bfloat16),
        scratch_shapes=[
            pltpu.VMEM((PAIRS, 2, half, MM), jnp.bfloat16),
            pltpu.VMEM(spectra.shape, jnp.bfloat16),
            pltpu.VMEM((2 * PAIRS, C, MM), jnp.bfloat16),
            pltpu.SemaphoreType.DMA((2 * PAIRS,)),
            pltpu.SemaphoreType.DMA((2 * PAIRS,)),
        ],
        compiler_params=pltpu.CompilerParams(vmem_limit_bytes=MEDIUM),
        cost_estimate=pl.CostEstimate(flops=8 * PAIRS * half * C * MM, bytes_accessed=8 * MIB, transcendentals=0),
    )(spectra, legendre, packed)


def by_lat(flat):
    return flat.reshape(-1, LATS, flat.shape[1]).transpose(1, 0, 2)


def shards(state, in_weight, in_bias, out_weight, out_bias, legendre):
    swap = [(0, 1), (1, 0)]
    flat = state.reshape(-1, HALF)
    received = [lax.ppermute(flat[:, :CHUNK], "lon", swap)]
    own, packed, *encoder = encode_own(
        by_lat(flat), *(
            pltpu.with_memory_space_constraint(array, pltpu.HBM)
            for array in (in_weight, in_bias, out_weight, out_bias, legendre)))
    rest, own = lax.optimization_barrier((flat[:, CHUNK:], own))
    received.append(lax.ppermute(rest, "lon", swap))
    first = first_lons(by_lat(received[0]), encoder, own)
    first, last = lax.optimization_barrier((first, received[1]))
    table = jnp.asarray(dft_tables()).astype(jnp.bfloat16)
    spectra = transform(by_lat(last), encoder, own, first, table)
    packed, spectra = lax.optimization_barrier((packed, spectra))
    packed = lax.ppermute(packed, "lon", swap)
    spectra = spectra.reshape(OWNERS, LATS, 2 * PAIRS * C)
    spectra = lax.all_to_all(spectra, ALL, split_axis=0, concat_axis=0, tiled=True, axis_index_groups=groups())
    result = contract(spectra.reshape(OWNERS * LATS, 2 * PAIRS * C), legendre, packed)
    return result.reshape(PAIRS, 2, 2, CH, MM).transpose(0, 1, 4, 2, 3)


def solution(mesh):
    return jax.shard_map(
        shards,
        mesh=mesh,
        in_specs=(P(None, "lat", "lon"), P(), P(), P(), P(), P("lat", None, "lon", None)),
        out_specs=P("lat", None, None, None, "lon"),
        check_vma=False,
    )
```

```python
import jax
import jax.numpy as jnp
import numpy as np
from jax import lax
from jax.experimental import pallas as pl
from jax.experimental.pallas import tpu as pltpu
from jax.sharding import PartitionSpec as P

NLON = 1024
HALF = NLON // 2
MM = 512
C = 384
CH = C // 2
OWNERS = 64
PAIRS = 4
LATS = 8
CHUNK = 384
LANE = 128
TOGETHER = 2
OWN_TOGETHER, FIRST_TOGETHER, REST_TOGETHER = 2, 2, 8
TILES = MM // LANE
KEPT = (TILES + 1) * LANE
SECOND_FROM = MM // 2
ALL = ("lat", "lon")
MIB = 1 << 20
SMALL = 16 * MIB
MEDIUM = 24 * MIB


def owner_bit(lat):
    return (lat // 2) % 2


PLACES = [4 * z + y for y in range(3, -1, -1) for z in range(3, -1, -1)]
BITS = (0, 1)
LISTED = [4 * place + 2 * bit + core for place in PLACES for bit in BITS for core in range(2)]


def groups():
    return [[2 * lat + (owner_bit(lat) ^ group) for lat in LISTED] for group in range(2)]


def my_group():
    return owner_bit(lax.axis_index("lat")) ^ lax.axis_index("lon")


def dft_tables():
    columns = np.arange(HALF)
    tables = []
    for parity in range(2):
        rows = []
        for bit in range(2):
            owner = np.array([lat for lat in LISTED if owner_bit(lat) == bit])
            for pair in range(PAIRS):
                index = PAIRS * owner + pair
                order = index if (pair + parity) % 2 == 0 else MM - 1 - index
                assert np.all(order % 2 == parity)
                phase = (order[:, None] * columns[None, :]) % NLON
                angle = phase * (2.0 * np.pi / NLON)
                rows += [np.cos(angle), -np.sin(angle)]
        tables.append(np.concatenate(rows) / np.sqrt(float(NLON)))
    return np.stack(tables).astype(np.float32)


def tile_place(packed_tile, block):
    in_first = packed_tile < TILES - block
    return jnp.where(in_first, 0, 1), jnp.where(in_first, block + packed_tile, packed_tile - 1)


def order_block():
    return (lax.axis_index("lat") * PAIRS) // LANE


def channel_order(array):
    pieces = [array[:, 0:128], array[:, 192:320], array[:, 128:192], array[:, 320:384]]
    zero = jnp.concatenate(pieces, axis=1)
    one = jnp.concatenate([pieces[1], pieces[0], pieces[3], pieces[2]], axis=1)
    return jnp.where(my_group() == 0, zero, one)


def encode_rows(x, w1, b1, w2, b2):
    hidden = lax.dot_general(x, w1, (((0,), (0,)), ((), ())), preferred_element_type=jnp.float32)
    hidden = hidden + b1
    hidden = (0.5 * hidden) * (1.0 + lax.erf(hidden * np.float32(np.sqrt(0.5))))
    features = jnp.dot(hidden.astype(jnp.bfloat16), w2, preferred_element_type=jnp.float32)
    return (features + b2).astype(jnp.bfloat16)


def pack_copies(legendre_ref, staged, sems):
    block = order_block()
    copies = []
    for tile in range(TILES + 1):
        member, source = tile_place(tile, block)
        lanes = pl.ds(pl.multiple_of(source * LANE, LANE), LANE)
        copies.append(pltpu.make_async_copy(
            legendre_ref.at[:, member, :, lanes],
            staged.at[:, :, tile * LANE:(tile + 1) * LANE],
            sems.at[tile],
        ))
    return copies


def encode_own_kernel(x_ref, w1_hbm, b1_hbm, w2_hbm, b2_hbm, legendre_ref,
                      features_ref, packed_ref, w1_ref, b1_ref, w2_ref, b2_ref,
                      b1_raw, w2_raw, b2_raw, staged, sems, loaded, sent):
    copies = pack_copies(legendre_ref, staged, sems)
    loads = [
        pltpu.make_async_copy(source, target, loaded.at[at])
        for at, (source, target) in enumerate(
            ((w1_hbm, w1_ref), (b1_hbm, b1_raw), (w2_hbm, w2_raw), (b2_hbm, b2_raw)))
    ]
    for load in loads:
        load.start()
    for copy in copies:
        copy.start()
    for load in loads:
        load.wait()
    b1_ref[...] = b1_raw[...][None, :]
    w2_ref[...] = channel_order(w2_raw[...])
    b2_ref[...] = channel_order(b2_raw[...][None, :])
    for lat, features in encode_lats(x_ref, w1_ref, b1_ref, w2_ref, b2_ref, OWN_TOGETHER):
        features_ref[lat] = features
    result = pltpu.make_async_copy(staged, packed_ref, sent)
    for copy in copies:
        copy.wait()
    result.start()
    result.wait()


def encode_lats(x_ref, w1_ref, b1_ref, w2_ref, b2_ref, together):
    lons = x_ref.shape[2]
    for lat in range(0, LATS, together):
        rows = jnp.concatenate([x_ref[lat + at] for at in range(together)], axis=1)
        features = encode_rows(rows, w1_ref[...], b1_ref[...], w2_ref[...], b2_ref[...])
        for at in range(together):
            yield lat + at, features[at * lons:(at + 1) * lons]


IN_VMEM = pl.BlockSpec(memory_space=pltpu.VMEM)
IN_HBM = pl.BlockSpec(memory_space=pltpu.HBM)


def encode_cost(lats, lons):
    return pl.CostEstimate(flops=2 * lats * lons * C * (C + 73), bytes_accessed=MIB,
                           transcendentals=lats * lons * C)


def combine(own, theirs):
    own, theirs = own.astype(jnp.float32), theirs.astype(jnp.float32)
    sign = jnp.where(lax.axis_index("lon") == 0, 1.0, -1.0)
    return (own + theirs).astype(jnp.bfloat16), (sign * (own - theirs)).astype(jnp.bfloat16)


def first_kernel(x_ref, w1_ref, b1_ref, w2_ref, b2_ref, own_ref, parts_ref):
    lons = x_ref.shape[2]
    for lat, theirs in encode_lats(x_ref, w1_ref, b1_ref, w2_ref, b2_ref, FIRST_TOGETHER):
        parts_ref[0, lat], parts_ref[1, lat] = combine(own_ref[lat, :lons], theirs)


def first_lons(x, encoder, own):
    lats, _, lons = x.shape
    return pl.pallas_call(
        first_kernel,
        in_specs=[IN_VMEM] * 6,
        out_specs=IN_VMEM,
        out_shape=pltpu.VMEM((2, lats, lons, C), jnp.bfloat16),
        compiler_params=pltpu.CompilerParams(vmem_limit_bytes=SMALL),
        cost_estimate=encode_cost(lats, lons),
    )(x, *encoder, own)


def encode_own(x, w1, b1, w2, b2, legendre):
    lats, _, lons = x.shape
    pairs, _, rows, _ = legendre.shape
    return pl.pallas_call(
        encode_own_kernel,
        in_specs=[IN_VMEM] + [IN_HBM] * 5,
        out_specs=[IN_VMEM, IN_HBM] + [IN_VMEM] * 4,
        out_shape=[
            pltpu.VMEM((lats, lons, C), jnp.bfloat16),
            pltpu.HBM((pairs, rows, KEPT), jnp.bfloat16),
            pltpu.VMEM(w1.shape, jnp.bfloat16),
            pltpu.VMEM((1, C), jnp.float32),
            pltpu.VMEM(w2.shape, jnp.bfloat16),
            pltpu.VMEM((1, C), jnp.float32),
        ],
        scratch_shapes=[
            pltpu.VMEM(b1.shape, jnp.float32),
            pltpu.VMEM(w2.shape, jnp.bfloat16),
            pltpu.VMEM(b2.shape, jnp.float32),
            pltpu.VMEM((pairs, rows, KEPT), jnp.bfloat16),
            pltpu.SemaphoreType.DMA((TILES + 1,)),
            pltpu.SemaphoreType.DMA((4,)),
            pltpu.SemaphoreType.DMA,
        ],
        compiler_params=pltpu.CompilerParams(vmem_limit_bytes=SMALL),
        cost_estimate=encode_cost(lats, lons),
    )(x, w1, b1, w2, b2, legendre)


def transform_kernel(x_ref, w1_ref, b1_ref, w2_ref, b2_ref, own_ref, first_ref, table_ref, out_ref,
                     rest, held, staged, sems):
    lons = x_ref.shape[2]
    for lat, theirs in encode_lats(x_ref, w1_ref, b1_ref, w2_ref, b2_ref, REST_TOGETHER):
        rest[0, lat], rest[1, lat] = combine(own_ref[lat, HALF - lons:], theirs)
    copies = []
    for block in range(4):
        parity, bit = block // 2, block % 2
        spectra_block(parity, bit, table_ref, (first_ref, rest), held.at[block])
        for pair in range(PAIRS):
            arrange(bit, held.at[block, pair], staged.at[block, pair])
            slot = parity * PAIRS + pair
            copies.append(pltpu.make_async_copy(
                staged.at[block, pair],
                out_ref.at[:, BITS.index(bit), :, :, slot * C:(slot + 1) * C],
                sems.at[block, pair],
            ))
            copies[-1].start()
    for copy in copies:
        copy.wait()


def spectra_block(parity, bit, table_ref, parts, held):
    owners = OWNERS // 2
    left = table_ref[parity, bit * 2 * PAIRS * owners:(bit + 1) * 2 * PAIRS * owners, :]
    for lat in range(LATS):
        right = jnp.concatenate([
            jnp.concatenate([part[parity, lat, :, bit * LANE:(bit + 1) * LANE], part[parity, lat, :, 2 * LANE:]], axis=1)
            for part in parts
        ], axis=0)
        result = jnp.dot(left, right, preferred_element_type=jnp.float32)
        rows = pl.ds(lat, owners, stride=LATS)
        for pair in range(PAIRS):
            for angle in range(2):
                start = (pair * 2 + angle) * owners
                for at in range(2):
                    held[pair, angle, at, rows, :] = result[start:start + owners, at * LANE:(at + 1) * LANE]


def arrange(bit, held, staged):
    real, imag = held[0, 1], held[1, 1]
    if bit == 0:
        imag = pltpu.roll(imag, 64, 1)
    else:
        real = pltpu.roll(real, 64, 1)
    lane = lax.broadcasted_iota(jnp.int32, real.shape, 1)
    for at, piece in enumerate((held[0, 0], held[1, 0], jnp.where(lane < 64, real, imag))):
        staged[:, :, :, at * LANE:(at + 1) * LANE] = piece.reshape(-1, 2, LATS, LANE).astype(jnp.bfloat16)


def transform(x, encoder, own, first, table):
    return pl.pallas_call(
        transform_kernel,
        in_specs=[IN_VMEM] * 8,
        out_specs=IN_HBM,
        out_shape=pltpu.HBM((OWNERS // 4, 2, 2, LATS, 2 * PAIRS * C), jnp.bfloat16),
        scratch_shapes=[
            pltpu.VMEM((2, LATS, x.shape[2], C), jnp.bfloat16),
            pltpu.VMEM((4, PAIRS, 2, 2, OWNERS // 2 * LATS, LANE), jnp.float32),
            pltpu.VMEM((4, PAIRS, OWNERS // 4, 2, LATS, C), jnp.bfloat16),
            pltpu.SemaphoreType.DMA((4, PAIRS)),
        ],
        compiler_params=pltpu.CompilerParams(vmem_limit_bytes=MEDIUM),
        cost_estimate=pl.CostEstimate(flops=2 * LATS * HALF * C * (C // 2 + 2 * MM), bytes_accessed=4 * MIB,
                                      transcendentals=LATS * (HALF - CHUNK) * C),
    )(x, *encoder, own, first, table)


def contract_kernel(spectra_ref, own_ref, packed_ref, out_ref, kept, spectra, staged, read, written):
    half = own_ref.shape[2]
    reads = []
    for slot in range(2 * PAIRS):
        lanes = slice(slot * C, (slot + 1) * C)
        reads.append(pltpu.make_async_copy(spectra_ref.at[:, lanes], spectra.at[:, lanes], read.at[slot]))
    for pair in range(PAIRS):
        reads[pair].start()
        reads[PAIRS + pair].start()
    assemble(own_ref, packed_ref, kept, half)
    writes = []
    for pair in range(PAIRS):
        index = lax.axis_index("lat") * PAIRS + pair
        if pair % TOGETHER == 0:
            for at in range(pair, pair + TOGETHER):
                reads[at].wait()
                reads[PAIRS + at].wait()
        for member in range(2):
            slot = (pair + member) % 2 * PAIRS + pair
            start = member * SECOND_FROM
            order = MM - 1 - index if member else index
            values = lax.dot_general(
                by_latitude(spectra, slot), kept[pair, member, :, start:],
                (((0,), (0,)), ((), ())), preferred_element_type=jnp.float32)
            degree = lax.broadcasted_iota(jnp.int32, values.shape, 1) + start
            values = jnp.where(degree >= order, values, 0.0).astype(jnp.bfloat16)
            for at, to, count in ((0, 0, 128), (128, 192, 128), (256, 128, 64), (320, 320, 64)):
                staged[slot, to:to + count, start:] = values[at:at + count]
            if start:
                staged[slot, :, :start] = jnp.zeros((C, start), jnp.bfloat16)
            writes.append(pltpu.make_async_copy(staged.at[slot], out_ref.at[pair, member], written.at[slot]))
            writes[-1].start()
    for write in writes:
        write.wait()


def assemble(own_ref, packed_ref, kept, half):
    side = lax.axis_index("lon")
    block = order_block()
    mine = pl.ds(pl.multiple_of(side * half, half), half)
    theirs = pl.ds(pl.multiple_of((1 - side) * half, half), half)
    for pair in range(PAIRS):
        for member in range(2):
            start = member * SECOND_FROM
            kept[pair, member, mine, start:] = own_ref[pair, member, :, start:]
            kept[pair, member, theirs, start:start + LANE] = jnp.zeros((half, LANE), jnp.bfloat16)
        for tile in range(TILES + 1):
            member, place = tile_place(tile, block)
            lanes = pl.ds(pl.multiple_of(place * LANE, LANE), LANE)
            kept[pair, member, theirs, lanes] = packed_ref[pair, :, tile * LANE:(tile + 1) * LANE]


def by_latitude(spectra, slot):
    starts = [LATS * LISTED.index(lat) for lat in range(0, OWNERS, 2)]
    return jnp.concatenate([spectra[start:start + 16, slot * C:(slot + 1) * C] for start in starts], axis=0)


def contract(spectra, legendre, packed):
    rows = spectra.shape[0]
    spectra = pltpu.with_memory_space_constraint(spectra, pltpu.HBM)
    return pl.pallas_call(
        contract_kernel,
        in_specs=[IN_HBM, IN_VMEM, IN_VMEM],
        out_specs=IN_HBM,
        out_shape=pltpu.HBM((PAIRS, 2, C, MM), jnp.bfloat16),
        scratch_shapes=[
            pltpu.VMEM((PAIRS, 2, rows, MM), jnp.bfloat16),
            pltpu.VMEM(spectra.shape, jnp.bfloat16),
            pltpu.VMEM((2 * PAIRS, C, MM), jnp.bfloat16),
            pltpu.SemaphoreType.DMA((2 * PAIRS,)),
            pltpu.SemaphoreType.DMA((2 * PAIRS,)),
        ],
        compiler_params=pltpu.CompilerParams(vmem_limit_bytes=MEDIUM),
        cost_estimate=pl.CostEstimate(flops=4 * PAIRS * rows * C * MM, bytes_accessed=8 * MIB, transcendentals=0),
    )(spectra, legendre, packed)


def by_lat(flat):
    return flat.reshape(-1, LATS, flat.shape[1]).transpose(1, 0, 2)


def shards(state, in_weight, in_bias, out_weight, out_bias, legendre):
    swap = [(0, 1), (1, 0)]
    flat = state.reshape(-1, HALF)
    received = [lax.ppermute(flat[:, :CHUNK], "lon", swap)]
    own, packed, *encoder = encode_own(
        by_lat(flat), *(
            pltpu.with_memory_space_constraint(array, pltpu.HBM)
            for array in (in_weight, in_bias, out_weight, out_bias, legendre)))
    rest, own = lax.optimization_barrier((flat[:, CHUNK:], own))
    received.append(lax.ppermute(rest, "lon", swap))
    first = first_lons(by_lat(received[0]), encoder, own)
    first, last = lax.optimization_barrier((first, received[1]))
    table = jnp.asarray(dft_tables()).astype(jnp.bfloat16)
    spectra = transform(by_lat(last), encoder, own, first, table)
    packed, spectra = lax.optimization_barrier((packed, spectra))
    packed = lax.ppermute(packed, "lon", swap)
    spectra = spectra.reshape(OWNERS, LATS, 2 * PAIRS * C)
    spectra = lax.all_to_all(spectra, ALL, split_axis=0, concat_axis=0, tiled=True, axis_index_groups=groups())
    result = contract(spectra.reshape(OWNERS * LATS, 2 * PAIRS * C), legendre, packed)
    return result.reshape(PAIRS, 2, 2, CH, MM).transpose(0, 1, 4, 2, 3)


def solution(mesh):
    return jax.shard_map(
        shards,
        mesh=mesh,
        in_specs=(P(None, "lat", "lon"), P(), P(), P(), P(), P("lat", None, "lon", None)),
        out_specs=P("lat", None, None, None, "lon"),
        check_vma=False,
    )
```

```python
import jax
import jax.numpy as jnp
import numpy as np
from jax import lax
from jax.experimental import pallas as pl
from jax.experimental.pallas import tpu as pltpu
from jax.sharding import PartitionSpec as P

NLON = 1024
HALF = NLON // 2
MM = 512
C = 384
CH = C // 2
OWNERS = 64
PAIRS = 4
LATS = 8
CHUNK = 384
LANE = 128
TOGETHER = 2
OWN_TOGETHER, FIRST_TOGETHER, REST_TOGETHER = 2, 2, 8
TILES = MM // LANE
KEPT = (TILES + 1) * LANE
SECOND_FROM = MM // 2
ALL = ("lat", "lon")
MIB = 1 << 20
SMALL = 16 * MIB
MEDIUM = 24 * MIB


def owner_bit(lat):
    return (lat // 2) % 2


PLACES = [4 * z + y for y in range(3, -1, -1) for z in range(3, -1, -1)]
BITS = (0, 1)
LISTED = [4 * place + 2 * bit + core for place in PLACES for bit in BITS for core in range(2)]


def groups():
    return [[2 * lat + (owner_bit(lat) ^ group) for lat in LISTED] for group in range(2)]


def my_group():
    return owner_bit(lax.axis_index("lat")) ^ lax.axis_index("lon")


def dft_tables():
    columns = np.arange(HALF)
    tables = []
    for parity in range(2):
        rows = []
        for bit in range(2):
            owner = np.array([lat for lat in LISTED if owner_bit(lat) == bit])
            for pair in range(PAIRS):
                index = PAIRS * owner + pair
                order = index if (pair + parity) % 2 == 0 else MM - 1 - index
                assert np.all(order % 2 == parity)
                phase = (order[:, None] * columns[None, :]) % NLON
                angle = phase * (2.0 * np.pi / NLON)
                rows += [np.cos(angle), -np.sin(angle)]
        tables.append(np.concatenate(rows) / np.sqrt(float(NLON)))
    return np.stack(tables).astype(np.float32)


def tile_place(packed_tile, block):
    in_first = packed_tile < TILES - block
    return jnp.where(in_first, 0, 1), jnp.where(in_first, block + packed_tile, packed_tile - 1)


def order_block():
    return (lax.axis_index("lat") * PAIRS) // LANE


def channel_order(array):
    pieces = [array[:, 0:128], array[:, 192:320], array[:, 128:192], array[:, 320:384]]
    zero = jnp.concatenate(pieces, axis=1)
    one = jnp.concatenate([pieces[1], pieces[0], pieces[3], pieces[2]], axis=1)
    return jnp.where(my_group() == 0, zero, one)


def encode_rows(x, w1, b1, w2, b2):
    hidden = lax.dot_general(x, w1, (((0,), (0,)), ((), ())), preferred_element_type=jnp.float32)
    hidden = hidden + b1
    hidden = (0.5 * hidden) * (1.0 + lax.erf(hidden * np.float32(np.sqrt(0.5))))
    features = jnp.dot(hidden.astype(jnp.bfloat16), w2, preferred_element_type=jnp.float32)
    return (features + b2).astype(jnp.bfloat16)


def pack_copies(legendre_ref, staged, sems):
    block = order_block()
    copies = []
    for tile in range(TILES + 1):
        member, source = tile_place(tile, block)
        lanes = pl.ds(pl.multiple_of(source * LANE, LANE), LANE)
        copies.append(pltpu.make_async_copy(
            legendre_ref.at[:, member, :, lanes],
            staged.at[:, :, tile * LANE:(tile + 1) * LANE],
            sems.at[tile],
        ))
    return copies


def encode_own_kernel(x_ref, w1_hbm, b1_hbm, w2_hbm, b2_hbm, legendre_ref,
                      features_ref, packed_ref, w1_ref, b1_ref, w2_ref, b2_ref,
                      b1_raw, w2_raw, b2_raw, staged, sems, loaded, sent):
    copies = pack_copies(legendre_ref, staged, sems)
    loads = [
        pltpu.make_async_copy(source, target, loaded.at[at])
        for at, (source, target) in enumerate(
            ((w1_hbm, w1_ref), (b1_hbm, b1_raw), (w2_hbm, w2_raw), (b2_hbm, b2_raw)))
    ]
    for load in loads:
        load.start()
    for copy in copies:
        copy.start()
    for load in loads:
        load.wait()
    b1_ref[...] = b1_raw[...][None, :]
    w2_ref[...] = channel_order(w2_raw[...])
    b2_ref[...] = channel_order(b2_raw[...][None, :])
    for lat, features in encode_lats(x_ref, w1_ref, b1_ref, w2_ref, b2_ref, OWN_TOGETHER):
        features_ref[lat] = features
    result = pltpu.make_async_copy(staged, packed_ref, sent)
    for copy in copies:
        copy.wait()
    result.start()
    result.wait()


def encode_lats(x_ref, w1_ref, b1_ref, w2_ref, b2_ref, together):
    lons = x_ref.shape[2]
    for lat in range(0, LATS, together):
        rows = jnp.concatenate([x_ref[lat + at] for at in range(together)], axis=1)
        features = encode_rows(rows, w1_ref[...], b1_ref[...], w2_ref[...], b2_ref[...])
        for at in range(together):
            yield lat + at, features[at * lons:(at + 1) * lons]


IN_VMEM = pl.BlockSpec(memory_space=pltpu.VMEM)
IN_HBM = pl.BlockSpec(memory_space=pltpu.HBM)


def encode_cost(lats, lons):
    return pl.CostEstimate(flops=2 * lats * lons * C * (C + 73), bytes_accessed=MIB,
                           transcendentals=lats * lons * C)


def combine(own, theirs):
    sign = jnp.where(lax.axis_index("lon") == 0, 1.0, -1.0).astype(jnp.bfloat16)
    return own + theirs, sign * (own - theirs)


def first_kernel(x_ref, w1_ref, b1_ref, w2_ref, b2_ref, own_ref, parts_ref):
    lons = x_ref.shape[2]
    for lat, theirs in encode_lats(x_ref, w1_ref, b1_ref, w2_ref, b2_ref, FIRST_TOGETHER):
        parts_ref[0, lat], parts_ref[1, lat] = combine(own_ref[lat, :lons], theirs)


def first_lons(x, encoder, own):
    lats, _, lons = x.shape
    return pl.pallas_call(
        first_kernel,
        in_specs=[IN_VMEM] * 6,
        out_specs=IN_VMEM,
        out_shape=pltpu.VMEM((2, lats, lons, C), jnp.bfloat16),
        compiler_params=pltpu.CompilerParams(vmem_limit_bytes=SMALL),
        cost_estimate=encode_cost(lats, lons),
    )(x, *encoder, own)


def encode_own(x, w1, b1, w2, b2, legendre):
    lats, _, lons = x.shape
    pairs, _, rows, _ = legendre.shape
    return pl.pallas_call(
        encode_own_kernel,
        in_specs=[IN_VMEM] + [IN_HBM] * 5,
        out_specs=[IN_VMEM, IN_HBM] + [IN_VMEM] * 4,
        out_shape=[
            pltpu.VMEM((lats, lons, C), jnp.bfloat16),
            pltpu.HBM((pairs, rows, KEPT), jnp.bfloat16),
            pltpu.VMEM(w1.shape, jnp.bfloat16),
            pltpu.VMEM((1, C), jnp.float32),
            pltpu.VMEM(w2.shape, jnp.bfloat16),
            pltpu.VMEM((1, C), jnp.float32),
        ],
        scratch_shapes=[
            pltpu.VMEM(b1.shape, jnp.float32),
            pltpu.VMEM(w2.shape, jnp.bfloat16),
            pltpu.VMEM(b2.shape, jnp.float32),
            pltpu.VMEM((pairs, rows, KEPT), jnp.bfloat16),
            pltpu.SemaphoreType.DMA((TILES + 1,)),
            pltpu.SemaphoreType.DMA((4,)),
            pltpu.SemaphoreType.DMA,
        ],
        compiler_params=pltpu.CompilerParams(vmem_limit_bytes=SMALL),
        cost_estimate=encode_cost(lats, lons),
    )(x, w1, b1, w2, b2, legendre)


def transform_kernel(x_ref, w1_ref, b1_ref, w2_ref, b2_ref, own_ref, first_ref, table_ref, out_ref,
                     rest, held, staged, sems):
    lons = x_ref.shape[2]
    for lat, theirs in encode_lats(x_ref, w1_ref, b1_ref, w2_ref, b2_ref, REST_TOGETHER):
        rest[0, lat], rest[1, lat] = combine(own_ref[lat, HALF - lons:], theirs)
    copies = []
    for block in range(4):
        parity, bit = block // 2, block % 2
        spectra_block(parity, bit, table_ref, (first_ref, rest), held.at[block])
        for pair in range(PAIRS):
            arrange(bit, held.at[block, pair], staged.at[block, pair])
            slot = parity * PAIRS + pair
            copies.append(pltpu.make_async_copy(
                staged.at[block, pair],
                out_ref.at[:, BITS.index(bit), :, :, slot * C:(slot + 1) * C],
                sems.at[block, pair],
            ))
            copies[-1].start()
    for copy in copies:
        copy.wait()


def spectra_block(parity, bit, table_ref, parts, held):
    owners = OWNERS // 2
    left = table_ref[parity, bit * 2 * PAIRS * owners:(bit + 1) * 2 * PAIRS * owners, :]
    for lat in range(LATS):
        right = jnp.concatenate([
            jnp.concatenate([part[parity, lat, :, bit * LANE:(bit + 1) * LANE], part[parity, lat, :, 2 * LANE:]], axis=1)
            for part in parts
        ], axis=0)
        result = jnp.dot(left, right, preferred_element_type=jnp.float32)
        rows = pl.ds(lat, owners, stride=LATS)
        for pair in range(PAIRS):
            for angle in range(2):
                start = (pair * 2 + angle) * owners
                for at in range(2):
                    held[pair, angle, at, rows, :] = result[start:start + owners, at * LANE:(at + 1) * LANE]


def arrange(bit, held, staged):
    real, imag = held[0, 1], held[1, 1]
    if bit == 0:
        imag = pltpu.roll(imag, 64, 1)
    else:
        real = pltpu.roll(real, 64, 1)
    lane = lax.broadcasted_iota(jnp.int32, real.shape, 1)
    for at, piece in enumerate((held[0, 0], held[1, 0], jnp.where(lane < 64, real, imag))):
        staged[:, :, :, at * LANE:(at + 1) * LANE] = piece.reshape(-1, 2, LATS, LANE).astype(jnp.bfloat16)


def transform(x, encoder, own, first, table):
    return pl.pallas_call(
        transform_kernel,
        in_specs=[IN_VMEM] * 8,
        out_specs=IN_HBM,
        out_shape=pltpu.HBM((OWNERS // 4, 2, 2, LATS, 2 * PAIRS * C), jnp.bfloat16),
        scratch_shapes=[
            pltpu.VMEM((2, LATS, x.shape[2], C), jnp.bfloat16),
            pltpu.VMEM((4, PAIRS, 2, 2, OWNERS // 2 * LATS, LANE), jnp.float32),
            pltpu.VMEM((4, PAIRS, OWNERS // 4, 2, LATS, C), jnp.bfloat16),
            pltpu.SemaphoreType.DMA((4, PAIRS)),
        ],
        compiler_params=pltpu.CompilerParams(vmem_limit_bytes=MEDIUM),
        cost_estimate=pl.CostEstimate(flops=2 * LATS * HALF * C * (C // 2 + 2 * MM), bytes_accessed=4 * MIB,
                                      transcendentals=LATS * (HALF - CHUNK) * C),
    )(x, *encoder, own, first, table)


def contract_kernel(spectra_ref, own_ref, packed_ref, out_ref, kept, spectra, staged, read, written):
    half = own_ref.shape[2]
    reads = []
    for slot in range(2 * PAIRS):
        lanes = slice(slot * C, (slot + 1) * C)
        reads.append(pltpu.make_async_copy(spectra_ref.at[:, lanes], spectra.at[:, lanes], read.at[slot]))
    for pair in range(PAIRS):
        reads[pair].start()
        reads[PAIRS + pair].start()
    assemble(own_ref, packed_ref, kept, half)
    writes = []
    for pair in range(PAIRS):
        index = lax.axis_index("lat") * PAIRS + pair
        if pair % TOGETHER == 0:
            for at in range(pair, pair + TOGETHER):
                reads[at].wait()
                reads[PAIRS + at].wait()
        for member in range(2):
            slot = (pair + member) % 2 * PAIRS + pair
            start = member * SECOND_FROM
            order = MM - 1 - index if member else index
            values = lax.dot_general(
                by_latitude(spectra, slot), kept[pair, member, :, start:],
                (((0,), (0,)), ((), ())), preferred_element_type=jnp.float32)
            degree = lax.broadcasted_iota(jnp.int32, values.shape, 1) + start
            values = jnp.where(degree >= order, values, 0.0).astype(jnp.bfloat16)
            for at, to, count in ((0, 0, 128), (128, 192, 128), (256, 128, 64), (320, 320, 64)):
                staged[slot, to:to + count, start:] = values[at:at + count]
            if start:
                staged[slot, :, :start] = jnp.zeros((C, start), jnp.bfloat16)
            writes.append(pltpu.make_async_copy(staged.at[slot], out_ref.at[pair, member], written.at[slot]))
            writes[-1].start()
    for write in writes:
        write.wait()


def assemble(own_ref, packed_ref, kept, half):
    side = lax.axis_index("lon")
    block = order_block()
    mine = pl.ds(pl.multiple_of(side * half, half), half)
    theirs = pl.ds(pl.multiple_of((1 - side) * half, half), half)
    for pair in range(PAIRS):
        for member in range(2):
            start = member * SECOND_FROM
            kept[pair, member, mine, start:] = own_ref[pair, member, :, start:]
            kept[pair, member, theirs, start:start + LANE] = jnp.zeros((half, LANE), jnp.bfloat16)
        for tile in range(TILES + 1):
            member, place = tile_place(tile, block)
            lanes = pl.ds(pl.multiple_of(place * LANE, LANE), LANE)
            kept[pair, member, theirs, lanes] = packed_ref[pair, :, tile * LANE:(tile + 1) * LANE]


def by_latitude(spectra, slot):
    starts = [LATS * LISTED.index(lat) for lat in range(0, OWNERS, 2)]
    return jnp.concatenate([spectra[start:start + 16, slot * C:(slot + 1) * C] for start in starts], axis=0)


def contract(spectra, legendre, packed):
    rows = spectra.shape[0]
    spectra = pltpu.with_memory_space_constraint(spectra, pltpu.HBM)
    return pl.pallas_call(
        contract_kernel,
        in_specs=[IN_HBM, IN_VMEM, IN_VMEM],
        out_specs=IN_HBM,
        out_shape=pltpu.HBM((PAIRS, 2, C, MM), jnp.bfloat16),
        scratch_shapes=[
            pltpu.VMEM((PAIRS, 2, rows, MM), jnp.bfloat16),
            pltpu.VMEM(spectra.shape, jnp.bfloat16),
            pltpu.VMEM((2 * PAIRS, C, MM), jnp.bfloat16),
            pltpu.SemaphoreType.DMA((2 * PAIRS,)),
            pltpu.SemaphoreType.DMA((2 * PAIRS,)),
        ],
        compiler_params=pltpu.CompilerParams(vmem_limit_bytes=MEDIUM),
        cost_estimate=pl.CostEstimate(flops=4 * PAIRS * rows * C * MM, bytes_accessed=8 * MIB, transcendentals=0),
    )(spectra, legendre, packed)


def by_lat(flat):
    return flat.reshape(-1, LATS, flat.shape[1]).transpose(1, 0, 2)


def shards(state, in_weight, in_bias, out_weight, out_bias, legendre):
    swap = [(0, 1), (1, 0)]
    flat = state.reshape(-1, HALF)
    received = [lax.ppermute(flat[:, :CHUNK], "lon", swap)]
    own, packed, *encoder = encode_own(
        by_lat(flat), *(
            pltpu.with_memory_space_constraint(array, pltpu.HBM)
            for array in (in_weight, in_bias, out_weight, out_bias, legendre)))
    rest, own = lax.optimization_barrier((flat[:, CHUNK:], own))
    received.append(lax.ppermute(rest, "lon", swap))
    first = first_lons(by_lat(received[0]), encoder, own)
    first, last = lax.optimization_barrier((first, received[1]))
    table = jnp.asarray(dft_tables()).astype(jnp.bfloat16)
    spectra = transform(by_lat(last), encoder, own, first, table)
    packed, spectra = lax.optimization_barrier((packed, spectra))
    packed = lax.ppermute(packed, "lon", swap)
    spectra = spectra.reshape(OWNERS, LATS, 2 * PAIRS * C)
    spectra = lax.all_to_all(spectra, ALL, split_axis=0, concat_axis=0, tiled=True, axis_index_groups=groups())
    result = contract(spectra.reshape(OWNERS * LATS, 2 * PAIRS * C), legendre, packed)
    return result.reshape(PAIRS, 2, 2, CH, MM).transpose(0, 1, 4, 2, 3)


def solution(mesh):
    return jax.shard_map(
        shards,
        mesh=mesh,
        in_specs=(P(None, "lat", "lon"), P(), P(), P(), P(), P("lat", None, "lon", None)),
        out_specs=P("lat", None, None, None, "lon"),
        check_vma=False,
    )
```

```python
import jax
import jax.numpy as jnp
import numpy as np
from jax import lax
from jax.experimental import pallas as pl
from jax.experimental.pallas import tpu as pltpu
from jax.sharding import PartitionSpec as P

NLON = 1024
HALF = NLON // 2
MM = 512
C = 384
CH = C // 2
OWNERS = 64
PAIRS = 4
LATS = 8
CHUNK = 384
LANE = 128
TOGETHER = 2
OWN_TOGETHER, FIRST_TOGETHER, REST_TOGETHER = 2, 2, 8
TILES = MM // LANE
KEPT = (TILES + 1) * LANE
SECOND_FROM = MM // 2
ALL = ("lat", "lon")
MIB = 1 << 20
SMALL = 16 * MIB
MEDIUM = 24 * MIB


def owner_bit(lat):
    return (lat // 2) % 2


PLACES = [4 * z + y for y in range(3, -1, -1) for z in range(3, -1, -1)]
BITS = (0, 1)
LISTED = [4 * place + 2 * bit + core for place in PLACES for bit in BITS for core in range(2)]


def groups():
    return [[2 * lat + (owner_bit(lat) ^ group) for lat in LISTED] for group in range(2)]


def my_group():
    return owner_bit(lax.axis_index("lat")) ^ lax.axis_index("lon")


def dft_tables():
    columns = np.arange(HALF)
    tables = []
    for parity in range(2):
        rows = []
        for bit in range(2):
            owner = np.array([lat for lat in LISTED if owner_bit(lat) == bit])
            for pair in range(PAIRS):
                index = PAIRS * owner + pair
                order = index if (pair + parity) % 2 == 0 else MM - 1 - index
                assert np.all(order % 2 == parity)
                phase = (order[:, None] * columns[None, :]) % NLON
                angle = phase * (2.0 * np.pi / NLON)
                rows += [np.cos(angle), -np.sin(angle)]
        tables.append(np.concatenate(rows) / np.sqrt(float(NLON)))
    return np.stack(tables).astype(np.float32)


def tile_place(packed_tile, block):
    in_first = packed_tile < TILES - block
    return jnp.where(in_first, 0, 1), jnp.where(in_first, block + packed_tile, packed_tile - 1)


def order_block():
    return (lax.axis_index("lat") * PAIRS) // LANE


def channel_order(array):
    pieces = [array[:, 0:128], array[:, 192:320], array[:, 128:192], array[:, 320:384]]
    zero = jnp.concatenate(pieces, axis=1)
    one = jnp.concatenate([pieces[1], pieces[0], pieces[3], pieces[2]], axis=1)
    return jnp.where(my_group() == 0, zero, one)


def encode_rows(x, w1, b1, w2, b2):
    hidden = lax.dot_general(x, w1, (((0,), (0,)), ((), ())), preferred_element_type=jnp.float32)
    hidden = hidden + b1
    hidden = (0.5 * hidden) * (1.0 + lax.erf(hidden * np.float32(np.sqrt(0.5))))
    features = jnp.dot(hidden.astype(jnp.bfloat16), w2, preferred_element_type=jnp.float32)
    return (features + b2).astype(jnp.bfloat16)


def pack_copies(legendre_ref, staged, sems):
    block = order_block()
    copies = []
    for tile in range(TILES + 1):
        member, source = tile_place(tile, block)
        lanes = pl.ds(pl.multiple_of(source * LANE, LANE), LANE)
        copies.append(pltpu.make_async_copy(
            legendre_ref.at[:, member, :, lanes],
            staged.at[:, :, tile * LANE:(tile + 1) * LANE],
            sems.at[tile],
        ))
    return copies


def encode_own_kernel(x_ref, w1_hbm, b1_hbm, w2_hbm, b2_hbm, legendre_ref,
                      features_ref, packed_ref, w1_ref, b1_ref, w2_ref, b2_ref,
                      b1_raw, w2_raw, b2_raw, staged, sems, loaded, sent):
    copies = pack_copies(legendre_ref, staged, sems)
    loads = [
        pltpu.make_async_copy(source, target, loaded.at[at])
        for at, (source, target) in enumerate(
            ((w1_hbm, w1_ref), (b1_hbm, b1_raw), (w2_hbm, w2_raw), (b2_hbm, b2_raw)))
    ]
    for load in loads:
        load.start()
    for copy in copies:
        copy.start()
    for load in loads:
        load.wait()
    b1_ref[...] = b1_raw[...][None, :]
    w2_ref[...] = channel_order(w2_raw[...])
    b2_ref[...] = channel_order(b2_raw[...][None, :])
    for lat, features in encode_lats(x_ref, w1_ref, b1_ref, w2_ref, b2_ref, OWN_TOGETHER):
        features_ref[lat] = features
    result = pltpu.make_async_copy(staged, packed_ref, sent)
    for copy in copies:
        copy.wait()
    result.start()
    result.wait()


def encode_lats(x_ref, w1_ref, b1_ref, w2_ref, b2_ref, together):
    lons = x_ref.shape[2]
    for lat in range(0, LATS, together):
        rows = jnp.concatenate([x_ref[lat + at] for at in range(together)], axis=1)
        features = encode_rows(rows, w1_ref[...], b1_ref[...], w2_ref[...], b2_ref[...])
        for at in range(together):
            yield lat + at, features[at * lons:(at + 1) * lons]


IN_VMEM = pl.BlockSpec(memory_space=pltpu.VMEM)
IN_HBM = pl.BlockSpec(memory_space=pltpu.HBM)


def encode_cost(lats, lons):
    return pl.CostEstimate(flops=2 * lats * lons * C * (C + 73), bytes_accessed=MIB,
                           transcendentals=lats * lons * C)


def combine(own, theirs):
    sign = jnp.where(lax.axis_index("lon") == 0, 1.0, -1.0).astype(jnp.bfloat16)
    return own + theirs, sign * (own - theirs)


def first_kernel(x_ref, w1_ref, b1_ref, w2_ref, b2_ref, own_ref, parts_ref):
    lons = x_ref.shape[2]
    for lat, theirs in encode_lats(x_ref, w1_ref, b1_ref, w2_ref, b2_ref, FIRST_TOGETHER):
        parts_ref[0, lat], parts_ref[1, lat] = combine(own_ref[lat, :lons], theirs)


def first_lons(x, encoder, own):
    lats, _, lons = x.shape
    return pl.pallas_call(
        first_kernel,
        in_specs=[IN_VMEM] * 6,
        out_specs=IN_VMEM,
        out_shape=pltpu.VMEM((2, lats, lons, C), jnp.bfloat16),
        compiler_params=pltpu.CompilerParams(vmem_limit_bytes=SMALL),
        cost_estimate=encode_cost(lats, lons),
    )(x, *encoder, own)


def encode_own(x, w1, b1, w2, b2, legendre):
    lats, _, lons = x.shape
    pairs, _, rows, _ = legendre.shape
    return pl.pallas_call(
        encode_own_kernel,
        in_specs=[IN_VMEM] + [IN_HBM] * 5,
        out_specs=[IN_VMEM, IN_HBM] + [IN_VMEM] * 4,
        out_shape=[
            pltpu.VMEM((lats, lons, C), jnp.bfloat16),
            pltpu.HBM((pairs, rows, KEPT), jnp.bfloat16),
            pltpu.VMEM(w1.shape, jnp.bfloat16),
            pltpu.VMEM((1, C), jnp.float32),
            pltpu.VMEM(w2.shape, jnp.bfloat16),
            pltpu.VMEM((1, C), jnp.float32),
        ],
        scratch_shapes=[
            pltpu.VMEM(b1.shape, jnp.float32),
            pltpu.VMEM(w2.shape, jnp.bfloat16),
            pltpu.VMEM(b2.shape, jnp.float32),
            pltpu.VMEM((pairs, rows, KEPT), jnp.bfloat16),
            pltpu.SemaphoreType.DMA((TILES + 1,)),
            pltpu.SemaphoreType.DMA((4,)),
            pltpu.SemaphoreType.DMA,
        ],
        compiler_params=pltpu.CompilerParams(vmem_limit_bytes=SMALL),
        cost_estimate=encode_cost(lats, lons),
    )(x, w1, b1, w2, b2, legendre)


def transform_kernel(x_ref, w1_ref, b1_ref, w2_ref, b2_ref, own_ref, first_ref, table_ref, out_ref,
                     rest, held, staged, sems):
    lons = x_ref.shape[2]
    for lat, theirs in encode_lats(x_ref, w1_ref, b1_ref, w2_ref, b2_ref, REST_TOGETHER):
        rest[0, lat], rest[1, lat] = combine(own_ref[lat, HALF - lons:], theirs)
    copies = []
    for block in range(4):
        parity, bit = block // 2, block % 2
        spectra_block(parity, bit, table_ref, (first_ref, rest), held.at[block])
        for pair in range(PAIRS):
            arrange(bit, held.at[block, pair], staged.at[block, pair])
            slot = parity * PAIRS + pair
            copies.append(pltpu.make_async_copy(
                staged.at[block, pair],
                out_ref.at[:, BITS.index(bit), :, slot * C:(slot + 1) * C],
                sems.at[block, pair],
            ))
            copies[-1].start()
    for copy in copies:
        copy.wait()


def spectra_block(parity, bit, table_ref, parts, held):
    owners = OWNERS // 2
    left = table_ref[parity, bit * 2 * PAIRS * owners:(bit + 1) * 2 * PAIRS * owners, :]
    for lat in range(LATS):
        right = jnp.concatenate([
            jnp.concatenate([part[parity, lat, :, bit * LANE:(bit + 1) * LANE], part[parity, lat, :, 2 * LANE:]], axis=1)
            for part in parts
        ], axis=0)
        result = jnp.dot(left, right, preferred_element_type=jnp.float32)
        rows = pl.ds(lat, owners, stride=LATS)
        for pair in range(PAIRS):
            for angle in range(2):
                start = (pair * 2 + angle) * owners
                for at in range(2):
                    held[pair, angle, at, rows, :] = result[start:start + owners, at * LANE:(at + 1) * LANE]


def arrange(bit, held, staged):
    real, imag = held[0, 1], held[1, 1]
    if bit == 0:
        imag = pltpu.roll(imag, 64, 1)
    else:
        real = pltpu.roll(real, 64, 1)
    lane = lax.broadcasted_iota(jnp.int32, real.shape, 1)
    for at, piece in enumerate((held[0, 0], held[1, 0], jnp.where(lane < 64, real, imag))):
        staged[:, :, at * LANE:(at + 1) * LANE] = piece.astype(jnp.bfloat16).reshape(-1, 2 * LATS, LANE)


def transform(x, encoder, own, first, table):
    return pl.pallas_call(
        transform_kernel,
        in_specs=[IN_VMEM] * 8,
        out_specs=IN_HBM,
        out_shape=pltpu.HBM((OWNERS // 4, 2, 2 * LATS, 2 * PAIRS * C), jnp.bfloat16),
        scratch_shapes=[
            pltpu.VMEM((2, LATS, x.shape[2], C), jnp.bfloat16),
            pltpu.VMEM((4, PAIRS, 2, 2, OWNERS // 2 * LATS, LANE), jnp.float32),
            pltpu.VMEM((4, PAIRS, OWNERS // 4, 2 * LATS, C), jnp.bfloat16),
            pltpu.SemaphoreType.DMA((4, PAIRS)),
        ],
        compiler_params=pltpu.CompilerParams(vmem_limit_bytes=MEDIUM),
        cost_estimate=pl.CostEstimate(flops=2 * LATS * HALF * C * (C // 2 + 2 * MM), bytes_accessed=4 * MIB,
                                      transcendentals=LATS * (HALF - CHUNK) * C),
    )(x, *encoder, own, first, table)


def contract_kernel(spectra_ref, own_ref, packed_ref, out_ref, kept, spectra, staged, read, written):
    half = own_ref.shape[2]
    reads = []
    for slot in range(2 * PAIRS):
        lanes = slice(slot * C, (slot + 1) * C)
        reads.append(pltpu.make_async_copy(spectra_ref.at[:, lanes], spectra.at[:, lanes], read.at[slot]))
    for pair in range(PAIRS):
        reads[pair].start()
        reads[PAIRS + pair].start()
    assemble(own_ref, packed_ref, kept, half)
    writes = []
    for pair in range(PAIRS):
        index = lax.axis_index("lat") * PAIRS + pair
        if pair % TOGETHER == 0:
            for at in range(pair, pair + TOGETHER):
                reads[at].wait()
                reads[PAIRS + at].wait()
        for member in range(2):
            slot = (pair + member) % 2 * PAIRS + pair
            start = member * SECOND_FROM
            order = MM - 1 - index if member else index
            values = lax.dot_general(
                by_latitude(spectra, slot), kept[pair, member, :, start:],
                (((0,), (0,)), ((), ())), preferred_element_type=jnp.float32)
            degree = lax.broadcasted_iota(jnp.int32, values.shape, 1) + start
            values = jnp.where(degree >= order, values, 0.0).astype(jnp.bfloat16)
            for at, to, count in ((0, 0, 128), (128, 192, 128), (256, 128, 64), (320, 320, 64)):
                staged[slot, to:to + count, start:] = values[at:at + count]
            if start:
                staged[slot, :, :start] = jnp.zeros((C, start), jnp.bfloat16)
            writes.append(pltpu.make_async_copy(staged.at[slot], out_ref.at[pair, member], written.at[slot]))
            writes[-1].start()
    for write in writes:
        write.wait()


def assemble(own_ref, packed_ref, kept, half):
    side = lax.axis_index("lon")
    block = order_block()
    mine = pl.ds(pl.multiple_of(side * half, half), half)
    theirs = pl.ds(pl.multiple_of((1 - side) * half, half), half)
    for pair in range(PAIRS):
        for member in range(2):
            start = member * SECOND_FROM
            kept[pair, member, mine, start:] = own_ref[pair, member, :, start:]
            kept[pair, member, theirs, start:start + LANE] = jnp.zeros((half, LANE), jnp.bfloat16)
        for tile in range(TILES + 1):
            member, place = tile_place(tile, block)
            lanes = pl.ds(pl.multiple_of(place * LANE, LANE), LANE)
            kept[pair, member, theirs, lanes] = packed_ref[pair, :, tile * LANE:(tile + 1) * LANE]


def by_latitude(spectra, slot):
    starts = [LATS * LISTED.index(lat) for lat in range(0, OWNERS, 2)]
    return jnp.concatenate([spectra[start:start + 16, slot * C:(slot + 1) * C] for start in starts], axis=0)


def contract(spectra, legendre, packed):
    rows = spectra.shape[0]
    spectra = pltpu.with_memory_space_constraint(spectra, pltpu.HBM)
    return pl.pallas_call(
        contract_kernel,
        in_specs=[IN_HBM, IN_VMEM, IN_VMEM],
        out_specs=IN_HBM,
        out_shape=pltpu.HBM((PAIRS, 2, C, MM), jnp.bfloat16),
        scratch_shapes=[
            pltpu.VMEM((PAIRS, 2, rows, MM), jnp.bfloat16),
            pltpu.VMEM(spectra.shape, jnp.bfloat16),
            pltpu.VMEM((2 * PAIRS, C, MM), jnp.bfloat16),
            pltpu.SemaphoreType.DMA((2 * PAIRS,)),
            pltpu.SemaphoreType.DMA((2 * PAIRS,)),
        ],
        compiler_params=pltpu.CompilerParams(vmem_limit_bytes=MEDIUM),
        cost_estimate=pl.CostEstimate(flops=4 * PAIRS * rows * C * MM, bytes_accessed=8 * MIB, transcendentals=0),
    )(spectra, legendre, packed)


def by_lat(flat):
    return flat.reshape(-1, LATS, flat.shape[1]).transpose(1, 0, 2)


def shards(state, in_weight, in_bias, out_weight, out_bias, legendre):
    swap = [(0, 1), (1, 0)]
    flat = state.reshape(-1, HALF)
    received = [lax.ppermute(flat[:, :CHUNK], "lon", swap)]
    own, packed, *encoder = encode_own(
        by_lat(flat), *(
            pltpu.with_memory_space_constraint(array, pltpu.HBM)
            for array in (in_weight, in_bias, out_weight, out_bias, legendre)))
    rest, own = lax.optimization_barrier((flat[:, CHUNK:], own))
    received.append(lax.ppermute(rest, "lon", swap))
    first = first_lons(by_lat(received[0]), encoder, own)
    first, last = lax.optimization_barrier((first, received[1]))
    table = jnp.asarray(dft_tables()).astype(jnp.bfloat16)
    spectra = transform(by_lat(last), encoder, own, first, table)
    packed, spectra = lax.optimization_barrier((packed, spectra))
    packed = lax.ppermute(packed, "lon", swap)
    spectra = spectra.reshape(OWNERS, LATS, 2 * PAIRS * C)
    spectra = lax.all_to_all(spectra, ALL, split_axis=0, concat_axis=0, tiled=True, axis_index_groups=groups())
    result = contract(spectra.reshape(OWNERS * LATS, 2 * PAIRS * C), legendre, packed)
    return result.reshape(PAIRS, 2, 2, CH, MM).transpose(0, 1, 4, 2, 3)


def solution(mesh):
    return jax.shard_map(
        shards,
        mesh=mesh,
        in_specs=(P(None, "lat", "lon"), P(), P(), P(), P(), P("lat", None, "lon", None)),
        out_specs=P("lat", None, None, None, "lon"),
        check_vma=False,
    )
```

```python
import jax
import jax.numpy as jnp
import numpy as np
from jax import lax
from jax.experimental import pallas as pl
from jax.experimental.pallas import tpu as pltpu
from jax.sharding import PartitionSpec as P

NLON = 1024
HALF = NLON // 2
MM = 512
C = 384
CH = C // 2
OWNERS = 64
PAIRS = 4
LATS = 8
CHUNK = 384
LANE = 128
TOGETHER = 2
OWN_TOGETHER, FIRST_TOGETHER, REST_TOGETHER = 2, 2, 8
TILES = MM // LANE
KEPT = (TILES + 1) * LANE
SECOND_FROM = MM // 2
ALL = ("lat", "lon")
MIB = 1 << 20
SMALL = 16 * MIB
MEDIUM = 24 * MIB


def owner_bit(lat):
    return (lat // 2) % 2


PLACES = [4 * z + y for y in range(3, -1, -1) for z in range(3, -1, -1)]
BITS = (0, 1)
LISTED = [4 * place + 2 * bit + core for place in PLACES for bit in BITS for core in range(2)]


def groups():
    return [[2 * lat + (owner_bit(lat) ^ group) for lat in LISTED] for group in range(2)]


def my_group():
    return owner_bit(lax.axis_index("lat")) ^ lax.axis_index("lon")


def dft_tables():
    columns = np.arange(HALF)
    tables = []
    for parity in range(2):
        rows = []
        for bit in range(2):
            owner = np.array([lat for lat in LISTED if owner_bit(lat) == bit])
            for pair in range(PAIRS):
                index = PAIRS * owner + pair
                order = index if (pair + parity) % 2 == 0 else MM - 1 - index
                assert np.all(order % 2 == parity)
                phase = (order[:, None] * columns[None, :]) % NLON
                angle = phase * (2.0 * np.pi / NLON)
                rows += [np.cos(angle), -np.sin(angle)]
        tables.append(np.concatenate(rows) / np.sqrt(float(NLON)))
    return np.stack(tables).astype(np.float32)


def tile_place(packed_tile, block):
    in_first = packed_tile < TILES - block
    return jnp.where(in_first, 0, 1), jnp.where(in_first, block + packed_tile, packed_tile - 1)


def order_block():
    return (lax.axis_index("lat") * PAIRS) // LANE


def channel_order(array):
    pieces = [array[:, 0:128], array[:, 192:320], array[:, 128:192], array[:, 320:384]]
    zero = jnp.concatenate(pieces, axis=1)
    one = jnp.concatenate([pieces[1], pieces[0], pieces[3], pieces[2]], axis=1)
    return jnp.where(my_group() == 0, zero, one)


def encode_rows(x, w1, b1, w2, b2):
    hidden = lax.dot_general(x, w1, (((0,), (0,)), ((), ())), preferred_element_type=jnp.float32)
    hidden = hidden + b1
    hidden = (0.5 * hidden) * (1.0 + lax.erf(hidden * np.float32(np.sqrt(0.5))))
    features = jnp.dot(hidden.astype(jnp.bfloat16), w2, preferred_element_type=jnp.float32)
    return (features + b2).astype(jnp.bfloat16)


def pack_copies(legendre_ref, staged, sems):
    block = order_block()
    copies = []
    for tile in range(TILES + 1):
        member, source = tile_place(tile, block)
        lanes = pl.ds(pl.multiple_of(source * LANE, LANE), LANE)
        copies.append(pltpu.make_async_copy(
            legendre_ref.at[:, member, :, lanes],
            staged.at[:, :, tile * LANE:(tile + 1) * LANE],
            sems.at[tile],
        ))
    return copies


def encode_own_kernel(x_ref, w1_hbm, b1_hbm, w2_hbm, b2_hbm, legendre_ref,
                      features_ref, packed_ref, w1_ref, b1_ref, w2_ref, b2_ref,
                      b1_raw, w2_raw, b2_raw, staged, sems, loaded, sent):
    copies = pack_copies(legendre_ref, staged, sems)
    loads = [
        pltpu.make_async_copy(source, target, loaded.at[at])
        for at, (source, target) in enumerate(
            ((w1_hbm, w1_ref), (b1_hbm, b1_raw), (w2_hbm, w2_raw), (b2_hbm, b2_raw)))
    ]
    for load in loads:
        load.start()
    for copy in copies:
        copy.start()
    for load in loads:
        load.wait()
    b1_ref[...] = b1_raw[...][None, :]
    w2_ref[...] = channel_order(w2_raw[...])
    b2_ref[...] = channel_order(b2_raw[...][None, :])
    for lat, features in encode_lats(x_ref, w1_ref, b1_ref, w2_ref, b2_ref, OWN_TOGETHER):
        features_ref[lat] = features
    result = pltpu.make_async_copy(staged, packed_ref, sent)
    for copy in copies:
        copy.wait()
    result.start()
    result.wait()


def encode_lats(x_ref, w1_ref, b1_ref, w2_ref, b2_ref, together):
    lons = x_ref.shape[2]
    for lat in range(0, LATS, together):
        rows = jnp.concatenate([x_ref[lat + at] for at in range(together)], axis=1)
        features = encode_rows(rows, w1_ref[...], b1_ref[...], w2_ref[...], b2_ref[...])
        for at in range(together):
            yield lat + at, features[at * lons:(at + 1) * lons]


IN_VMEM = pl.BlockSpec(memory_space=pltpu.VMEM)
IN_HBM = pl.BlockSpec(memory_space=pltpu.HBM)


def encode_cost(lats, lons):
    return pl.CostEstimate(flops=2 * lats * lons * C * (C + 73), bytes_accessed=MIB,
                           transcendentals=lats * lons * C)


def combine(own, theirs):
    sign = jnp.where(lax.axis_index("lon") == 0, 1.0, -1.0).astype(jnp.bfloat16)
    return own + theirs, sign * (own - theirs)


def first_kernel(x_ref, w1_ref, b1_ref, w2_ref, b2_ref, own_ref, parts_ref):
    lons = x_ref.shape[2]
    for lat, theirs in encode_lats(x_ref, w1_ref, b1_ref, w2_ref, b2_ref, FIRST_TOGETHER):
        parts_ref[0, lat], parts_ref[1, lat] = combine(own_ref[lat, :lons], theirs)


def first_lons(x, encoder, own):
    lats, _, lons = x.shape
    return pl.pallas_call(
        first_kernel,
        in_specs=[IN_VMEM] * 6,
        out_specs=IN_VMEM,
        out_shape=pltpu.VMEM((2, lats, lons, C), jnp.bfloat16),
        compiler_params=pltpu.CompilerParams(vmem_limit_bytes=SMALL),
        cost_estimate=encode_cost(lats, lons),
    )(x, *encoder, own)


def encode_own(x, w1, b1, w2, b2, legendre):
    lats, _, lons = x.shape
    pairs, _, rows, _ = legendre.shape
    return pl.pallas_call(
        encode_own_kernel,
        in_specs=[IN_VMEM] + [IN_HBM] * 5,
        out_specs=[IN_VMEM, IN_HBM] + [IN_VMEM] * 4,
        out_shape=[
            pltpu.VMEM((lats, lons, C), jnp.bfloat16),
            pltpu.HBM((pairs, rows, KEPT), jnp.bfloat16),
            pltpu.VMEM(w1.shape, jnp.bfloat16),
            pltpu.VMEM((1, C), jnp.float32),
            pltpu.VMEM(w2.shape, jnp.bfloat16),
            pltpu.VMEM((1, C), jnp.float32),
        ],
        scratch_shapes=[
            pltpu.VMEM(b1.shape, jnp.float32),
            pltpu.VMEM(w2.shape, jnp.bfloat16),
            pltpu.VMEM(b2.shape, jnp.float32),
            pltpu.VMEM((pairs, rows, KEPT), jnp.bfloat16),
            pltpu.SemaphoreType.DMA((TILES + 1,)),
            pltpu.SemaphoreType.DMA((4,)),
            pltpu.SemaphoreType.DMA,
        ],
        compiler_params=pltpu.CompilerParams(vmem_limit_bytes=SMALL),
        cost_estimate=encode_cost(lats, lons),
    )(x, w1, b1, w2, b2, legendre)


def transform_kernel(x_ref, w1_ref, b1_ref, w2_ref, b2_ref, own_ref, first_ref, table_ref, out_ref,
                     rest, held, staged, sems):
    lons = x_ref.shape[2]
    for lat, theirs in encode_lats(x_ref, w1_ref, b1_ref, w2_ref, b2_ref, REST_TOGETHER):
        rest[0, lat], rest[1, lat] = combine(own_ref[lat, HALF - lons:], theirs)
    copies = []
    for block in range(4):
        parity, bit = block // 2, block % 2
        spectra_block(parity, bit, table_ref, (first_ref, rest), held.at[block])
        for pair in range(PAIRS):
            arrange(bit, held.at[block, pair], staged.at[block, pair])
            slot = parity * PAIRS + pair
            copies.append(pltpu.make_async_copy(
                staged.at[block, pair],
                out_ref.at[:, BITS.index(bit), :, slot * C:(slot + 1) * C],
                sems.at[block, pair],
            ))
            copies[-1].start()
    for copy in copies:
        copy.wait()


def spectra_block(parity, bit, table_ref, parts, held):
    owners = OWNERS // 2
    left = table_ref[parity, bit * 2 * PAIRS * owners:(bit + 1) * 2 * PAIRS * owners, :]
    for lat in range(LATS):
        right = jnp.concatenate([
            jnp.concatenate([part[parity, lat, :, bit * LANE:(bit + 1) * LANE], part[parity, lat, :, 2 * LANE:]], axis=1)
            for part in parts
        ], axis=0)
        result = jnp.dot(left, right, preferred_element_type=jnp.float32)
        rows = pl.ds(lat, owners, stride=LATS)
        for pair in range(PAIRS):
            for angle in range(2):
                start = (pair * 2 + angle) * owners
                for at in range(2):
                    held[pair, angle, at, rows, :] = result[start:start + owners, at * LANE:(at + 1) * LANE]


def arrange(bit, held, staged):
    real, imag = held[0, 1], held[1, 1]
    if bit == 0:
        imag = pltpu.roll(imag, 64, 1)
    else:
        real = pltpu.roll(real, 64, 1)
    lane = lax.broadcasted_iota(jnp.int32, real.shape, 1)
    for at, piece in enumerate((held[0, 0], held[1, 0], jnp.where(lane < 64, real, imag))):
        staged[:, :, at * LANE:(at + 1) * LANE] = piece.astype(jnp.bfloat16).reshape(-1, 2 * LATS, LANE)


def transform(x, encoder, own, first, table):
    return pl.pallas_call(
        transform_kernel,
        in_specs=[IN_VMEM] * 8,
        out_specs=IN_HBM,
        out_shape=pltpu.HBM((OWNERS // 4, 2, 2 * LATS, 2 * PAIRS * C), jnp.bfloat16),
        scratch_shapes=[
            pltpu.VMEM((2, LATS, x.shape[2], C), jnp.bfloat16),
            pltpu.VMEM((4, PAIRS, 2, 2, OWNERS // 2 * LATS, LANE), jnp.float32),
            pltpu.VMEM((4, PAIRS, OWNERS // 4, 2 * LATS, C), jnp.bfloat16),
            pltpu.SemaphoreType.DMA((4, PAIRS)),
        ],
        compiler_params=pltpu.CompilerParams(vmem_limit_bytes=MEDIUM),
        cost_estimate=pl.CostEstimate(flops=2 * LATS * HALF * C * (C // 2 + 2 * MM), bytes_accessed=4 * MIB,
                                      transcendentals=LATS * (HALF - CHUNK) * C),
    )(x, *encoder, own, first, table)


def contract_kernel(spectra_ref, own_ref, packed_ref, out_ref, kept, spectra, staged, read, written):
    half = own_ref.shape[2]
    reads = []
    for slot in range(2 * PAIRS):
        lanes = slice(slot * C, (slot + 1) * C)
        reads.append(pltpu.make_async_copy(spectra_ref.at[:, lanes], spectra.at[:, lanes], read.at[slot]))
    for pair in range(PAIRS):
        reads[pair].start()
        reads[PAIRS + pair].start()
    assemble(own_ref, packed_ref, kept, half)
    writes = []
    for pair in range(PAIRS):
        index = lax.axis_index("lat") * PAIRS + pair
        if pair % TOGETHER == 0:
            for at in range(pair, pair + TOGETHER):
                reads[at].wait()
                reads[PAIRS + at].wait()
        for member in range(2):
            slot = (pair + member) % 2 * PAIRS + pair
            start = member * SECOND_FROM
            order = MM - 1 - index if member else index
            values = lax.dot_general(
                by_latitude(spectra, slot), kept[pair, member, :, start:],
                (((0,), (0,)), ((), ())), preferred_element_type=jnp.float32)
            degree = lax.broadcasted_iota(jnp.int32, (C, SECOND_FROM), 1) + start
            kept_values = jnp.where(degree >= order, values[:, :SECOND_FROM], 0.0).astype(jnp.bfloat16)
            if member == 0:
                kept_values = jnp.concatenate([kept_values, values[:, SECOND_FROM:].astype(jnp.bfloat16)], axis=1)
            values = kept_values
            for at, to, count in ((0, 0, 128), (128, 192, 128), (256, 128, 64), (320, 320, 64)):
                staged[slot, to:to + count, start:] = values[at:at + count]
            if start:
                staged[slot, :, :start] = jnp.zeros((C, start), jnp.bfloat16)
            writes.append(pltpu.make_async_copy(staged.at[slot], out_ref.at[pair, member], written.at[slot]))
            writes[-1].start()
    for write in writes:
        write.wait()


def assemble(own_ref, packed_ref, kept, half):
    side = lax.axis_index("lon")
    block = order_block()
    mine = pl.ds(pl.multiple_of(side * half, half), half)
    theirs = pl.ds(pl.multiple_of((1 - side) * half, half), half)
    for pair in range(PAIRS):
        for member in range(2):
            start = member * SECOND_FROM
            kept[pair, member, mine, start:] = own_ref[pair, member, :, start:]
            kept[pair, member, theirs, start:start + LANE] = jnp.zeros((half, LANE), jnp.bfloat16)
        for tile in range(TILES + 1):
            member, place = tile_place(tile, block)
            lanes = pl.ds(pl.multiple_of(place * LANE, LANE), LANE)
            kept[pair, member, theirs, lanes] = packed_ref[pair, :, tile * LANE:(tile + 1) * LANE]


def by_latitude(spectra, slot):
    starts = [LATS * LISTED.index(lat) for lat in range(0, OWNERS, 2)]
    return jnp.concatenate([spectra[start:start + 16, slot * C:(slot + 1) * C] for start in starts], axis=0)


def contract(spectra, legendre, packed):
    rows = spectra.shape[0]
    spectra = pltpu.with_memory_space_constraint(spectra, pltpu.HBM)
    return pl.pallas_call(
        contract_kernel,
        in_specs=[IN_HBM, IN_VMEM, IN_VMEM],
        out_specs=IN_HBM,
        out_shape=pltpu.HBM((PAIRS, 2, C, MM), jnp.bfloat16),
        scratch_shapes=[
            pltpu.VMEM((PAIRS, 2, rows, MM), jnp.bfloat16),
            pltpu.VMEM(spectra.shape, jnp.bfloat16),
            pltpu.VMEM((2 * PAIRS, C, MM), jnp.bfloat16),
            pltpu.SemaphoreType.DMA((2 * PAIRS,)),
            pltpu.SemaphoreType.DMA((2 * PAIRS,)),
        ],
        compiler_params=pltpu.CompilerParams(vmem_limit_bytes=MEDIUM),
        cost_estimate=pl.CostEstimate(flops=4 * PAIRS * rows * C * MM, bytes_accessed=8 * MIB, transcendentals=0),
    )(spectra, legendre, packed)


def by_lat(flat):
    return flat.reshape(-1, LATS, flat.shape[1]).transpose(1, 0, 2)


def shards(state, in_weight, in_bias, out_weight, out_bias, legendre):
    swap = [(0, 1), (1, 0)]
    flat = state.reshape(-1, HALF)
    received = [lax.ppermute(flat[:, :CHUNK], "lon", swap)]
    own, packed, *encoder = encode_own(
        by_lat(flat), *(
            pltpu.with_memory_space_constraint(array, pltpu.HBM)
            for array in (in_weight, in_bias, out_weight, out_bias, legendre)))
    rest, own = lax.optimization_barrier((flat[:, CHUNK:], own))
    received.append(lax.ppermute(rest, "lon", swap))
    first = first_lons(by_lat(received[0]), encoder, own)
    first, last = lax.optimization_barrier((first, received[1]))
    table = jnp.asarray(dft_tables()).astype(jnp.bfloat16)
    spectra = transform(by_lat(last), encoder, own, first, table)
    packed, spectra = lax.optimization_barrier((packed, spectra))
    packed = lax.ppermute(packed, "lon", swap)
    spectra = spectra.reshape(OWNERS, LATS, 2 * PAIRS * C)
    spectra = lax.all_to_all(spectra, ALL, split_axis=0, concat_axis=0, tiled=True, axis_index_groups=groups())
    result = contract(spectra.reshape(OWNERS * LATS, 2 * PAIRS * C), legendre, packed)
    return result.reshape(PAIRS, 2, 2, CH, MM).transpose(0, 1, 4, 2, 3)


def solution(mesh):
    return jax.shard_map(
        shards,
        mesh=mesh,
        in_specs=(P(None, "lat", "lon"), P(), P(), P(), P(), P("lat", None, "lon", None)),
        out_specs=P("lat", None, None, None, "lon"),
        check_vma=False,
    )
```
